32 devices in a mesh: grp: 4 (over z), seq: 8 (over y, x, core).
Axes of the slice: x: 2, y: 2, z: 4, core: 2. Of those that a mesh axis runs over, the one named last changes fastest.
Arguments:
- tokens: bfloat16 [32768, 512], P(('grp', 'seq')), may hold values from -6 to 6
- norm_gain1: float32 [512], replicated, may hold values from 0.5 to 1.5
- w_xz: bfloat16 [512, 2048], replicated, may hold values from -0.25 to 0.25
- w_bc: bfloat16 [512, 256], replicated, may hold values from -0.0234375 to 0.0234375
- w_dt: bfloat16 [512, 16], replicated, may hold values from -0.25 to 0.25
- dt_bias: float32 [16], replicated, may hold values from -1 to 1
- decay_rate: float32 [16], replicated, may hold values from 1.5258789e-06 to 0.08
- curve_jump: float32 [32768], P(('grp', 'seq')), may hold values from 0 to 1.4
- skip_gain: float32 [16], replicated, may hold values from 0.3 to 1
- norm_gain2: float32 [1024], replicated, may hold values from 0.5 to 1.5
- w_out: bfloat16 [1024, 512], replicated, may hold values from -0.1875 to 0.1875
- norm_gain3: float32 [512], replicated, may hold values from 0.5 to 1.5
- w_q: bfloat16 [512, 1024], replicated, may hold values from -15.909903 to 15.909903
- w_kv: bfloat16 [512, 2048], replicated, may hold values from -0.25 to 0.25
- w_o: bfloat16 [1024, 512], replicated, may hold values from -0.1875 to 0.1875
- nbr_owner: int32 [512, 2], P(('grp', 'seq')), may hold values from 0 to 7, all different within a row; in each aligned block of 16 rows (0 to 15, 16 to 31, ...) at most 4 rows name the same one
- nbr_block: int32 [512, 2], P(('grp', 'seq')), may hold values from 0 to 15
Outputs:
- layer_out: bfloat16 [32768, 512], P(('grp', 'seq'))
The draws below stay inside these ranges and needn't reach their ends.
Inputs may be any that keep to these rules, and one draw needn't show every extreme that they name: `nbr_owner`: no two slots of one block name the same owner; among the lists of one device's 16 blocks no owner is named more than 4 times, and in every draw some device names one owner exactly 4 times.
All inputs are finite; a program needn't handle non-finite values.
Results may differ from the reference program's by a relative error of at most 0.023.
Values may be sent and summed in bfloat16 or wider, within the bound.
A program may use at most 192 MiB of HBM per device.

```python
import math
import jax
import jax.numpy as jnp
import numpy as np
from jax import lax

D = 512
H = 16
P_SIZE = 64
NS = 128
INNER = 1024
CH = 128
BL = 64
KN = 2
TOK_DEV = 1024
BLK_DEV = 16
CAP = 4
TOKENS = 32768
NBLK = 512
N_GRP = 4
N_SEQ = 8


def draw_decay_rate(key, part):
    first, second, third = jax.random.split(key, 3)
    slow_heads = jax.random.randint(first, (H,), 0, 2) > 0
    slow_rate = jnp.exp(jax.random.uniform(second, (H,), jnp.float32, math.log(0.05), math.log(0.4))) / TOKENS
    fast_rate = jnp.exp(jax.random.uniform(third, (H,), jnp.float32, math.log(0.03), math.log(0.08)))
    return jnp.where(slow_heads, slow_rate, fast_rate).astype(jnp.float32)


def draw_curve_jump(key, part):
    first, second, third, fourth = jax.random.split(key, 4)
    device_count = TOKENS // TOK_DEV
    device_level = jnp.exp(jax.random.uniform(first, (device_count,), jnp.float32, math.log(0.1), 0.0))
    token_level = jnp.exp(jax.random.uniform(second, (TOKENS,), jnp.float32, math.log(0.5), math.log(2.0)))
    baseline = jnp.repeat(device_level, TOK_DEV) * token_level / TOKENS
    places = jax.random.randint(third, (6,), 0, TOKENS)
    amounts = jax.random.uniform(fourth, (6,), jnp.float32, 0.22, 0.69)
    return baseline.at[places].add(amounts).astype(jnp.float32)


def draw_w_q(key, part):
    first = jax.random.fold_in(key, 0)
    baseline = jnp.clip(jax.random.normal(first, (D, H * P_SIZE), jnp.float32), -6.0, 6.0) / math.sqrt(D)
    return baseline.astype(jnp.bfloat16)


def plant(values, rng, smallest, largest):
    spot = [jax.random.randint(jax.random.fold_in(rng, axis), (), 0, length) for axis, length in enumerate(values.shape)]
    main_axis = values.shape.index(max(values.shape))
    neighbour = spot[:main_axis] + [(spot[main_axis] + 1) % values.shape[main_axis]] + spot[main_axis + 1:]
    return values.at[tuple(spot)].set(smallest).at[tuple(neighbour)].set(largest)


def level_of(stream_key, extent, shards, smallest, top_value):
    level, own = 1.0, jax.random.fold_in(stream_key, 6)
    for dim, parts in shards:
        draws = jnp.exp(jax.random.uniform(jax.random.fold_in(own, dim), (parts,), jnp.float32, smallest / len(shards), top_value / len(shards)))
        level = level * jnp.repeat(draws, extent[dim] // parts).reshape([-1 if axis == dim else 1 for axis in range(len(extent))])
    return level


def shared_out(key, own, number, rows, amount, top, reach, lean):
    sequence = jax.random.permutation(key, amount)
    packed, common = load_shares(amount, rows * top, reach, lean, True), load_shares(amount, rows * top, reach, lean, False)
    places = jnp.arange(amount)

    def named(sizes, turn):
        used = int((sizes > 0).sum())
        fixed = max(1, used // 4)
        shifted = fixed + (places - fixed + turn * (used - fixed)) % max(1, amount - fixed)
        return jnp.zeros((amount,), jnp.int32).at[sequence[jnp.where(places < fixed, places, shifted)]].set(jnp.asarray(sizes, jnp.int32))

    sizes = jnp.where(number % 4 == 0, named(packed, number // 4), named(common, number - number // 4 - 1))
    mixed = jax.random.permutation(jax.random.fold_in(own, 3), amount)
    donor, sink = mixed[0:amount // 2 * 2:2], mixed[1:amount // 2 * 2:2]
    margin = jnp.minimum(sizes[donor] - 1, reach - sizes[sink]) // 2
    margin = jnp.where((donor == sequence[0]) | (sink == sequence[0]) | (sizes[sink] == 0), 0, jnp.maximum(margin, 0))
    shifted = jax.random.randint(jax.random.fold_in(own, 4), (amount // 2,), 0, 1 << 20) % (margin + 1)
    sizes = sizes.at[donor].add(-shifted).at[sink].add(shifted)
    labels = jnp.searchsorted(jnp.cumsum(sizes), jnp.arange(rows * top), side="right").astype(jnp.int32)
    grid = labels.reshape(top, rows).T
    grid = grid[jax.random.permutation(jax.random.fold_in(own, 1), rows)]
    turn = jax.random.randint(jax.random.fold_in(own, 2), (rows, 1), 0, top)
    return jnp.take_along_axis(grid, (jnp.arange(top)[None, :] + turn) % top, axis=1)


def load_shares(number_of, total, bound, skew, full):
    weights = [(1 << 20) // math.isqrt(grade ** skew) + 1 for grade in range(1, number_of + 1)]
    largest = bound if full else min(bound, max(-(-total // number_of), total * weights[0] // sum(weights)))
    least = 1 if total - largest >= number_of - 1 else 0
    given, surplus = [largest] + [least] * (number_of - 1), total - largest - least * (number_of - 1)
    while surplus > 0:
        movable = [i for i in range(1, number_of) if given[i] < largest] or [i for i in range(1, number_of) if given[i] < bound]
        pool, left = sum([weights[i] for i in movable]), surplus
        for i in movable:
            more = min(bound - given[i], max(1, left * weights[i] // pool), surplus)
            given[i] = given[i] + more
            surplus = surplus - more
    return np.array(given)


def noise(rng, shape, scale, reach, shards=(), held_as=jnp.bfloat16):
    array = jax.random.normal(rng, shape, jnp.float32) * scale
    if len(shards) > 0:
        array = level_of(rng, shape, shards, -0.22, 0.18) * array
    return jnp.clip(array, min=-reach, max=reach).astype(held_as)


def setup_inputs(seed: int = 0) -> dict:
    seeds = jax.random.split(jax.random.key(seed), 18)
    tokens = noise(seeds[0], (TOKENS, D), 1.0, 6.0, ((0, 32),))
    norm_gain1 = jnp.clip(jax.random.uniform(seeds[1], (D,), jnp.float32, 0.5, 1.5), 0.5, 1.5)
    w_xz = noise(seeds[2], (D, 2 * INNER), D ** -0.5, 0.25)
    w_bc = noise(seeds[3], (D, 2 * NS), (D * NS) ** -0.5, 0.0234375)
    w_dt = noise(seeds[4], (D, H), D ** -0.5, 0.25)
    dt_bias = jnp.clip(jax.random.uniform(seeds[5], (H,), jnp.float32, -1.0, 1.0), -1.0, 1.0)
    decay_rate = draw_decay_rate(jax.random.fold_in(seeds[17], 71), 0)
    curve_jump = draw_curve_jump(jax.random.fold_in(seeds[17], 71), 0)
    skip_gain = jnp.clip(jax.random.uniform(seeds[8], (H,), jnp.float32, 0.3, 1.0), 0.3, 1.0)
    norm_gain2 = jnp.clip(jax.random.uniform(seeds[9], (INNER,), jnp.float32, 0.5, 1.5), 0.5, 1.5)
    w_out = noise(seeds[10], (INNER, D), INNER ** -0.5, 0.1875)
    norm_gain3 = jnp.clip(jax.random.uniform(seeds[11], (D,), jnp.float32, 0.5, 1.5), 0.5, 1.5)
    w_q = draw_w_q(jax.random.fold_in(seeds[17], 71), 0)
    w_kv = noise(seeds[13], (D, 2 * INNER), D ** -0.5, 0.25)
    w_o = noise(seeds[14], (INNER, D), INNER ** -0.5, 0.1875)
    nbr_owner_keys = jax.random.split(jax.random.fold_in(seeds[15], 1), NBLK // BLK_DEV)
    nbr_owner_turns = jax.random.permutation(jax.random.fold_in(seeds[15], 3), NBLK // BLK_DEV)
    nbr_owner = jax.vmap(lambda own, number: shared_out(jax.random.fold_in(seeds[15], 2), own, number, BLK_DEV, N_SEQ, KN, CAP, 2))(nbr_owner_keys, nbr_owner_turns).reshape((NBLK, KN))
    nbr_block = plant(jax.random.randint(seeds[16], (NBLK, KN), 0, BLK_DEV), jax.random.fold_in(seeds[16], 1), 0, BLK_DEV - 1).astype(jnp.int32)
    return dict(tokens=tokens, norm_gain1=norm_gain1, w_xz=w_xz, w_bc=w_bc, w_dt=w_dt, dt_bias=dt_bias, decay_rate=decay_rate, curve_jump=curve_jump, skip_gain=skip_gain, norm_gain2=norm_gain2, w_out=w_out, norm_gain3=norm_gain3, w_q=w_q, w_kv=w_kv, w_o=w_o, nbr_owner=nbr_owner, nbr_block=nbr_block)


epsilon = 1e-05
highest = lax.Precision.HIGHEST

def rms_rows(values, weights):
    floats = values.astype(jnp.float32)
    return (floats * lax.rsqrt(lax.optimization_barrier(jnp.mean(floats * floats, axis=-1, keepdims=True)) + epsilon) * weights).astype(jnp.bfloat16)

def mamba_inputs(rows_in, norm_gain1, w_xz, w_bc, w_dt, dt_bias, decay_rate, jump_rows):
    normed = rms_rows(rows_in, norm_gain1)
    stream_gate = jnp.dot(normed, w_xz, preferred_element_type=jnp.float32).astype(jnp.bfloat16)
    maps = jnp.dot(normed, w_bc, preferred_element_type=jnp.float32).astype(jnp.bfloat16)
    step_size = jax.nn.softplus(jnp.dot(normed, w_dt, preferred_element_type=jnp.float32) + dt_bias)
    log_decay = -(decay_rate * step_size + jump_rows[:, None])
    return (stream_gate[:, :INNER], stream_gate[:, INNER:], maps[:, :NS], maps[:, NS:], step_size, log_decay)

def rounded_floats(values):
    return lax.optimization_barrier(values.astype(jnp.bfloat16)).astype(jnp.float32)

def state_scan(stream, input_map, output_map, step_size, log_decay, initial):
    count = stream.shape[0] // CH
    streams = stream.reshape(count, CH, H, P_SIZE)
    inputs = input_map.reshape(count, CH, NS)
    outputs = output_map.reshape(count, CH, NS)
    steps = step_size.reshape(count, CH, H)
    decays = log_decay.reshape(count, CH, H)
    lower = (jnp.arange(CH)[:, None] >= jnp.arange(CH)[None, :])[None]

    def advance(carried, pieces):
        block_x, block_b, block_c, block_u, block_l = pieces
        x_floats = block_x.astype(jnp.float32)
        running = jnp.cumsum(block_l, axis=0)
        across = running.T
        spread = across[:, :, None] - across[:, None, :]
        weights = jnp.where(lower, jnp.exp(jnp.where(lower, spread, 0.0)), 0.0)
        intersection = jnp.dot(block_c, block_b.T, preferred_element_type=jnp.float32)
        mixing = rounded_floats(intersection[None] * weights * block_u.T[:, None, :])
        result = jnp.einsum('hts,shp->thp', mixing, x_floats)
        result = result + jnp.exp(running)[:, :, None] * jnp.einsum('tn,hpn->thp', block_c.astype(jnp.float32), carried, precision=highest)
        tail_weight = jnp.exp(running[-1][None, :] - running) * block_u
        tail = rounded_floats(tail_weight[:, :, None] * x_floats)
        updated = jnp.exp(running[-1])[:, None, None] * carried + jnp.einsum('shp,sn->hpn', tail, block_b.astype(jnp.float32))
        return (updated, result)
    final, results = lax.scan(advance, initial, (streams, inputs, outputs, steps, decays))
    return (results.reshape(count * CH, H, P_SIZE), final)

def mamba_finish(rows_in, mixed_state, stream, gate_in, skip_gain, norm_gain2, w_out):
    total = mixed_state + skip_gain[None, :, None] * stream.astype(jnp.float32).reshape(-1, H, P_SIZE)
    gated = total * jax.nn.silu(gate_in.astype(jnp.float32)).reshape(-1, H, P_SIZE)
    normed = gated * lax.rsqrt(lax.optimization_barrier(jnp.mean(gated * gated, axis=-1, keepdims=True)) + epsilon)
    scaled = (normed.reshape(-1, INNER) * norm_gain2).astype(jnp.bfloat16)
    return (rows_in.astype(jnp.float32) + jnp.dot(scaled, w_out, preferred_element_type=jnp.float32)).astype(jnp.bfloat16)

def attend_blocks(queries, own_keys, own_values, far_keys, far_values):
    score_scale = 1.0 / math.sqrt(P_SIZE)
    query_floats = queries.astype(jnp.float32)
    own_scores = jnp.einsum('bqhd,bkhd->bhqk', query_floats, own_keys.astype(jnp.float32)) * score_scale
    far_scores = jnp.einsum('bqhd,bkhd->bhqk', query_floats, far_keys.astype(jnp.float32)) * score_scale
    peak = jnp.maximum(lax.optimization_barrier(jnp.max(own_scores, axis=-1, keepdims=True)), lax.optimization_barrier(jnp.max(far_scores, axis=-1, keepdims=True)))
    own_exp = jnp.exp(own_scores - peak)
    far_exp = jnp.exp(far_scores - peak)
    denominator = lax.optimization_barrier(jnp.sum(own_exp, axis=-1, keepdims=True)) + lax.optimization_barrier(jnp.sum(far_exp, axis=-1, keepdims=True))
    own_weight = (own_exp / denominator).astype(jnp.bfloat16)
    far_weight = (far_exp / denominator).astype(jnp.bfloat16)
    mixed = jnp.einsum('bhqk,bkhd->bqhd', own_weight.astype(jnp.float32), own_values.astype(jnp.float32))
    mixed = mixed + jnp.einsum('bhqk,bkhd->bqhd', far_weight.astype(jnp.float32), far_values.astype(jnp.float32))
    return mixed.astype(jnp.bfloat16)

def reference(tokens, norm_gain1, w_xz, w_bc, w_dt, dt_bias, decay_rate, curve_jump, skip_gain, norm_gain2, w_out, norm_gain3, w_q, w_kv, w_o, nbr_owner, nbr_block):
    devices = N_GRP * N_SEQ
    token_rows = tokens.reshape(devices, TOK_DEV, D)
    jump_rows = curve_jump.reshape(devices, TOK_DEV)

    def one_device(carried, pieces):
        rows_in, jumps = pieces
        stream, gate_in, input_map, output_map, step_size, log_decay = mamba_inputs(rows_in, norm_gain1, w_xz, w_bc, w_dt, dt_bias, decay_rate, jumps)
        mixed_state, updated = state_scan(stream, input_map, output_map, step_size, log_decay, carried)
        return (updated, mamba_finish(rows_in, mixed_state, stream, gate_in, skip_gain, norm_gain2, w_out))
    start = jnp.zeros((H, P_SIZE, NS), jnp.float32)
    _, middle = lax.scan(one_device, start, (token_rows, jump_rows))
    normed_all = lax.map(lambda rows: rms_rows(rows, norm_gain3), middle)
    key_value = lax.map(lambda rows: jnp.dot(rows, w_kv, preferred_element_type=jnp.float32).astype(jnp.bfloat16), normed_all)
    key_value = key_value.reshape(devices * BLK_DEV, BL, 2 * INNER)

    def attend_device(index):
        normed = normed_all[index]
        queries = jnp.dot(normed, w_q, preferred_element_type=jnp.float32).astype(jnp.bfloat16).reshape(BLK_DEV, BL, H, P_SIZE)
        first = (index * BLK_DEV).astype(jnp.int32)
        own = lax.dynamic_slice_in_dim(key_value, first, BLK_DEV, 0)
        owners = lax.dynamic_slice_in_dim(nbr_owner, first, BLK_DEV, 0)
        blocks = lax.dynamic_slice_in_dim(nbr_block, first, BLK_DEV, 0)
        global_ids = ((index // N_SEQ * N_SEQ + owners) * BLK_DEV + blocks).astype(jnp.int32)
        far = key_value[global_ids.reshape(-1)].reshape(BLK_DEV, KN * BL, 2 * INNER)
        attended = attend_blocks(queries, own[..., :INNER].reshape(BLK_DEV, BL, H, P_SIZE), own[..., INNER:].reshape(BLK_DEV, BL, H, P_SIZE), far[..., :INNER].reshape(BLK_DEV, KN * BL, H, P_SIZE), far[..., INNER:].reshape(BLK_DEV, KN * BL, H, P_SIZE)).reshape(TOK_DEV, INNER)
        return (middle[index].astype(jnp.float32) + jnp.dot(attended, w_o, preferred_element_type=jnp.float32)).astype(jnp.bfloat16)
    result = lax.map(attend_device, jnp.arange(devices, dtype=jnp.int32))
    return result.reshape(TOKENS, D)
```

```python
import functools
import math

import jax
import jax.numpy as jnp
from jax import lax
from jax.experimental import pallas as pl
from jax.experimental.pallas import tpu as pltpu
from jax.sharding import PartitionSpec as P

H = 16
P_SIZE = 64
NS = 128
INNER = 1024
CH = 128
BL = 64
KN = 2
PAIRS = INNER // 128
ROWS = 16
EPS = 1e-05
VMEM_LIMIT = 56 * 1024 * 1024
MESH = pl.DeviceIdType.MESH
F32 = jnp.float32
BF16 = jnp.bfloat16


def dot(a, b):
    return jnp.dot(a, b, preferred_element_type=F32)


def dot_nt(a, b):
    return lax.dot_general(a, b, (((1,), (1,)), ((), ())), preferred_element_type=F32)


def dot_tn(a, b):
    return lax.dot_general(a, b, (((0,), (0,)), ((), ())), preferred_element_type=F32)


def rms_rows(values, weights):
    floats = values.astype(F32)
    scale = lax.rsqrt(jnp.mean(floats * floats, axis=-1, keepdims=True) + EPS)
    return (floats * scale * weights).astype(BF16)


def split3(values):
    high = values.astype(BF16)
    rest = values - high.astype(F32)
    middle = rest.astype(BF16)
    low = (rest - middle.astype(F32)).astype(BF16)
    return jnp.concatenate([high, middle, low], axis=0)


def head_spread():
    head = lax.broadcasted_iota(jnp.int32, (3 * H, INNER), 0) % H
    lane = lax.broadcasted_iota(jnp.int32, (3 * H, INNER), 1) // P_SIZE
    return (head == lane).astype(BF16)


def local_kernel(
    tokens_ref, gain_ref, w_xz_ref, w_bc_ref, w_dt_ref, bias_ref, rate_ref, jump_ref,
    xz_ref, maps_ref, intra_ref, reach_ref, state_ref, factor_ref, total_ref, final_ref,
    carried, product,
):
    step = pl.program_id(0)
    chunks = tokens_ref.shape[0] // CH

    @pl.when(step == 0)
    def _():
        carried[...] = jnp.zeros_like(carried)
        product[...] = jnp.ones_like(product)

    normed = rms_rows(tokens_ref[...], gain_ref[...])
    xz_ref[...] = dot(normed, w_xz_ref[...]).astype(BF16)
    maps_ref[...] = dot(normed, w_bc_ref[...]).astype(BF16)
    steps_t = jax.nn.softplus(
        lax.dot_general(
            w_dt_ref[...], normed, (((0,), (1,)), ((), ())), preferred_element_type=F32
        )
        + bias_ref[...]
    )
    row = lax.broadcasted_iota(jnp.int32, (CH, CH), 0)
    col = lax.broadcasted_iota(jnp.int32, (CH, CH), 1)
    lower = row >= col
    upto = (row <= col).astype(F32)
    spread = head_spread()
    first_half = lax.broadcasted_iota(jnp.int32, (CH, 128), 1) < P_SIZE
    for c in range(chunks):
        rows = slice(c * CH, (c + 1) * CH)
        u_t = steps_t[:, rows]
        decay_t = -(rate_ref[...] * u_t + jump_ref[c])
        run_t = jnp.dot(decay_t, upto, precision=lax.Precision.HIGHEST, preferred_element_type=F32)
        run = jnp.concatenate([run_t, jnp.zeros((CH - H, CH), F32)], axis=0).T
        reach_t = jnp.exp(run_t)
        tail_t = jnp.exp(run_t[:, CH - 1 :] - run_t) * u_t
        reach_ref[:, rows] = reach_t
        tail_weight = dot_tn(split3(tail_t), spread)
        last = dot_tn(split3(reach_t[:, CH - 8 :]), spread)[7:8]
        b = maps_ref[rows, :NS]
        cmap = maps_ref[rows, NS:]
        crossing = dot_nt(cmap, b)
        for p in range(PAIRS):
            lanes = slice(p * 128, (p + 1) * 128)
            x = xz_ref[rows, lanes]
            parts = []
            for h in (2 * p, 2 * p + 1):
                gap = run[:, h : h + 1] - run_t[h : h + 1, :]
                weight = jnp.exp(jnp.where(lower, gap, -1e30))
                parts.append((crossing * weight * u_t[h : h + 1, :]).astype(BF16))
            zero = jnp.zeros_like(x)
            stacked = jnp.concatenate(
                [jnp.where(first_half, x, zero), jnp.where(first_half, zero, x)], axis=0
            )
            intra_ref[rows, lanes] = dot(jnp.concatenate(parts, axis=1), stacked)
        state_ref[c] = carried[...]
        factor_ref[c] = jnp.broadcast_to(product[...], (8, INNER))
        tail = (tail_weight * xz_ref[rows, :INNER].astype(F32)).astype(BF16)
        carried[...] = last * carried[...] + dot_tn(b, tail)
        product[...] = product[...] * last

    @pl.when(step == pl.num_programs(0) - 1)
    def _():
        final_ref[...] = carried[...].astype(BF16)
        for i in range(8):
            total_ref[i : i + 1, :] = product[:, i * 128 : (i + 1) * 128]


def local_part(tokens, gain, w_xz, w_bc, w_dt, bias, rate, jump):
    count = tokens.shape[0]
    tile = 2 * CH
    chunks = count // CH
    whole = lambda *shape: pl.BlockSpec(shape, lambda i: (0,) * len(shape))
    return pl.pallas_call(
        local_kernel,
        grid=(count // tile,),
        in_specs=[
            pl.BlockSpec((tile, 512), lambda i: (i, 0)),
            whole(1, 512),
            whole(512, 2 * INNER),
            whole(512, 2 * NS),
            whole(512, H),
            whole(H, 1),
            whole(H, 1),
            pl.BlockSpec((2, 1, CH), lambda i: (i, 0, 0)),
        ],
        out_specs=[
            pl.BlockSpec((tile, 2 * INNER), lambda i: (i, 0)),
            pl.BlockSpec((tile, 2 * NS), lambda i: (i, 0)),
            pl.BlockSpec((tile, INNER), lambda i: (i, 0)),
            pl.BlockSpec((H, tile), lambda i: (0, i)),
            pl.BlockSpec((2, NS, INNER), lambda i: (i, 0, 0)),
            pl.BlockSpec((2, 8, INNER), lambda i: (i, 0, 0)),
            whole(8, 128),
            whole(NS, INNER),
        ],
        out_shape=[
            jax.ShapeDtypeStruct((count, 2 * INNER), BF16),
            jax.ShapeDtypeStruct((count, 2 * NS), BF16),
            jax.ShapeDtypeStruct((count, INNER), F32),
            jax.ShapeDtypeStruct((H, count), F32),
            jax.ShapeDtypeStruct((chunks, NS, INNER), F32),
            jax.ShapeDtypeStruct((chunks, 8, INNER), F32),
            jax.ShapeDtypeStruct((8, 128), F32),
            jax.ShapeDtypeStruct((NS, INNER), BF16),
        ],
        scratch_shapes=[pltpu.VMEM((NS, INNER), F32), pltpu.VMEM((1, INNER), F32)],
        compiler_params=pltpu.CompilerParams(vmem_limit_bytes=VMEM_LIMIT),
        name="local_part",
    )(tokens, gain, w_xz, w_bc, w_dt, bias, rate, jump)


def greet(n_grp, n_seq, grp, seq):
    barrier = pltpu.get_barrier_semaphore()
    for d in range(1, n_seq):
        pl.semaphore_signal(
            barrier, inc=1, device_id=(grp, lax.rem(seq + d, n_seq)), device_id_type=MESH
        )
    for d in range(1, n_grp):
        pl.semaphore_signal(
            barrier, inc=1, device_id=(lax.rem(grp + d, n_grp), seq), device_id_type=MESH
        )
    pl.semaphore_wait(barrier, n_seq + n_grp - 2)


def prefix_kernel(
    n_grp, n_seq, state_ref, total_ref, wanted_ref, before_ref, asked_ref,
    parts, factors, sums, group_factor, shares, group_sum, my_factor, factor_row,
    send1, recv1, send2, recv2, send3, recv3, send4, recv4, send5, recv5, send6, recv6,
):
    grp, seq = lax.axis_index("grp"), lax.axis_index("seq")
    width = parts.shape[-1]
    greet(n_grp, n_seq, grp, seq)
    peers = [lax.rem(seq + d, n_seq) for d in range(n_seq)]
    origins = [lax.rem(seq + n_seq - d, n_seq) for d in range(n_seq)]
    layers = [lax.rem(grp + d, n_grp) for d in range(n_grp)]

    def across(src, dst, send, recv, d):
        return pltpu.make_async_remote_copy(
            src_ref=src, dst_ref=dst, send_sem=send.at[d], recv_sem=recv.at[d],
            device_id=(grp, peers[d]), device_id_type=MESH,
        )

    def along(src, dst, send, recv, d):
        return pltpu.make_async_remote_copy(
            src_ref=src, dst_ref=dst, send_sem=send.at[d], recv_sem=recv.at[d],
            device_id=(layers[d], seq), device_id_type=MESH,
        )

    first = []
    for d in range(1, n_seq):
        first.append(across(state_ref.at[peers[d]], parts.at[seq], send1, recv1, d))
        first.append(across(total_ref, factors.at[seq], send2, recv2, d))
    for copy in first:
        copy.start()
    asking = []
    for d in range(1, n_seq):
        asking.append(across(wanted_ref.at[peers[d]], asked_ref.at[seq], send3, recv3, d))
        asking[-1].start()
    parts[seq] = state_ref[seq]
    factors[seq] = total_ref[...]
    asked_ref[seq] = wanted_ref[seq]
    for copy in first:
        copy.wait()

    lanes = pl.ds(pl.multiple_of(lax.rem(seq, INNER // width) * width, width), width)

    def row_of(tile):
        for i in range(8):
            factor_row[:, i * 128 : (i + 1) * 128] = tile[i : i + 1, :]
        return factor_row[:, lanes]

    running = jnp.zeros((ROWS, width), F32)
    product = jnp.ones((8, 128), F32)
    for k in range(n_seq):
        sums[k] = running
        group_factor[k] = product
        running = row_of(factors[k]) * running + parts[k].astype(F32)
        product = product * factors[k]
    group_sum[grp] = running.astype(BF16)
    my_factor[grp] = product
    second = []
    for d in range(1, n_grp):
        second.append(along(group_sum.at[grp], group_sum.at[grp], send4, recv4, d))
        second.append(along(my_factor.at[grp], my_factor.at[grp], send5, recv5, d))
    for copy in second:
        copy.start()
    for copy in second:
        copy.wait()
    carry = jnp.zeros((ROWS, width), F32)
    for g in range(n_grp):
        new = row_of(my_factor[g]) * carry + group_sum[g].astype(F32)
        carry = jnp.where(g < grp, new, carry)
    for k in range(n_seq):
        shares[k] = (sums[k] + row_of(group_factor[k]) * carry).astype(BF16)
    third = []
    for d in range(1, n_seq):
        third.append(across(shares.at[peers[d]], before_ref.at[seq], send6, recv6, d))
        third[-1].start()
    before_ref[seq] = shares[seq]
    for copy in third:
        copy.wait()
    for copy in asking:
        copy.wait()


def prefix_part(state, total, wanted, n_grp, n_seq):
    spots = n_seq // 8
    width = INNER // spots
    sliced = state.reshape(8, ROWS, spots, width).swapaxes(1, 2).reshape(n_seq, ROWS, width)
    vmem = pl.BlockSpec(memory_space=pltpu.VMEM)
    dma = pltpu.SemaphoreType.DMA
    before, asked = pl.pallas_call(
        functools.partial(prefix_kernel, n_grp, n_seq),
        in_specs=[vmem] * 3,
        out_specs=[vmem] * 2,
        out_shape=[
            jax.ShapeDtypeStruct((n_seq, ROWS, width), BF16),
            jax.ShapeDtypeStruct(wanted.shape, jnp.int32),
        ],
        scratch_shapes=[
            pltpu.VMEM((n_seq, ROWS, width), BF16),
            pltpu.VMEM((n_seq, 8, 128), F32),
            pltpu.VMEM((n_seq, ROWS, width), F32),
            pltpu.VMEM((n_seq, 8, 128), F32),
            pltpu.VMEM((n_seq, ROWS, width), BF16),
            pltpu.VMEM((n_grp, ROWS, width), BF16),
            pltpu.VMEM((n_grp, 8, 128), F32),
            pltpu.VMEM((1, INNER), F32),
        ]
        + [dma((n_seq,))] * 6
        + [dma((n_grp,))] * 4
        + [dma((n_seq,))] * 2,
        compiler_params=pltpu.CompilerParams(
            collective_id=0, has_side_effects=True, vmem_limit_bytes=VMEM_LIMIT
        ),
        name="prefix_part",
    )(sliced, total, wanted)
    before = before.reshape(8, spots, ROWS, width).swapaxes(1, 2).reshape(NS, INNER)
    return before, asked


def finish_kernel(
    tokens_ref, xz_ref, maps_ref, intra_ref, reach_ref, state_ref, factor_ref, before_ref,
    skip_ref, gain2_ref, w_out_ref, gain3_ref, mid_ref, normed_ref, scaled,
):
    chunks = tokens_ref.shape[0] // CH
    spread = head_spread()
    group = lax.broadcasted_iota(jnp.int32, (256, 256), 0) // P_SIZE
    other = lax.broadcasted_iota(jnp.int32, (256, 256), 1) // P_SIZE
    same = (group == other).astype(BF16)
    for c in range(chunks):
        rows = slice(c * CH, (c + 1) * CH)
        state = state_ref[c] + factor_ref[c, 0:1] * before_ref[...].astype(F32)
        high = state.astype(BF16)
        low = (state - high.astype(F32)).astype(BF16)
        cmap = maps_ref[rows, NS:]
        reached = dot(
            jnp.concatenate([cmap, cmap], axis=1), jnp.concatenate([high, low], axis=0)
        )
        reach = dot_tn(split3(reach_ref[:, rows]), spread)
        mixed = intra_ref[rows] + reach * reached
        x = xz_ref[rows, :INNER].astype(F32)
        gate = xz_ref[rows, INNER:].astype(F32)
        gated = (mixed + skip_ref[...] * x) * (gate * jax.nn.sigmoid(gate))
        squares = (gated * gated).astype(BF16)
        power = jnp.concatenate(
            [dot(squares[:, i * 256 : (i + 1) * 256], same) for i in range(INNER // 256)], axis=1
        )
        scaled[rows] = (
            gated * lax.rsqrt(power * (1.0 / P_SIZE) + EPS) * gain2_ref[...]
        ).astype(BF16)
    middle = (tokens_ref[...].astype(F32) + dot(scaled[...], w_out_ref[...])).astype(BF16)
    mid_ref[...] = middle
    normed_ref[...] = rms_rows(middle, gain3_ref[...])


def finish_part(tokens, xz, maps, intra, reach, state, factor, before, skip, gain2, w_out, gain3):
    count = tokens.shape[0]
    tile = 2 * CH
    whole = lambda *shape: pl.BlockSpec(shape, lambda i: (0,) * len(shape))
    return pl.pallas_call(
        finish_kernel,
        grid=(count // tile,),
        in_specs=[
            pl.BlockSpec((tile, 512), lambda i: (i, 0)),
            pl.BlockSpec((tile, 2 * INNER), lambda i: (i, 0)),
            pl.BlockSpec((tile, 2 * NS), lambda i: (i, 0)),
            pl.BlockSpec((tile, INNER), lambda i: (i, 0)),
            pl.BlockSpec((H, tile), lambda i: (0, i)),
            pl.BlockSpec((2, NS, INNER), lambda i: (i, 0, 0)),
            pl.BlockSpec((2, 8, INNER), lambda i: (i, 0, 0)),
            whole(NS, INNER),
            whole(1, INNER),
            whole(1, INNER),
            whole(INNER, 512),
            whole(1, 512),
        ],
        out_specs=[pl.BlockSpec((tile, 512), lambda i: (i, 0))] * 2,
        out_shape=[jax.ShapeDtypeStruct((count, 512), BF16)] * 2,
        scratch_shapes=[pltpu.VMEM((tile, INNER), BF16)],
        compiler_params=pltpu.CompilerParams(vmem_limit_bytes=VMEM_LIMIT),
        name="finish_part",
    )(tokens, xz, maps, intra, reach, state, factor, before, skip, gain2, w_out, gain3)


def swap_kernel(n_seq, slots, asked_ref, normed_ref, arrived_ref, staged, send, recv, local):
    grp, seq = lax.axis_index("grp"), lax.axis_index("seq")
    barrier = pltpu.get_barrier_semaphore()
    for d in range(1, n_seq):
        pl.semaphore_signal(
            barrier, inc=1, device_id=(grp, lax.rem(seq + d, n_seq)), device_id_type=MESH
        )
    pl.semaphore_wait(barrier, n_seq - 1)
    copies = []
    for d in range(1, n_seq):
        peer = lax.rem(seq + d, n_seq)
        for j in range(slots):
            staged[d, j] = normed_ref[asked_ref[peer, j]]
        copies.append(
            pltpu.make_async_remote_copy(
                src_ref=staged.at[d], dst_ref=arrived_ref.at[seq],
                send_sem=send.at[d], recv_sem=recv.at[d],
                device_id=(grp, peer), device_id_type=MESH,
            )
        )
        copies[-1].start()
    for j in range(slots):
        staged[0, j] = normed_ref[asked_ref[seq, j]]
    own = pltpu.make_async_copy(staged.at[0], arrived_ref.at[seq], local)
    own.start()
    for copy in copies:
        copy.wait()
    own.wait()


def swap_part(asked, normed, n_seq):
    slots = asked.shape[1]
    vmem = pl.BlockSpec(memory_space=pltpu.VMEM)
    shape = (n_seq, slots, BL, 512)
    return pl.pallas_call(
        functools.partial(swap_kernel, n_seq, slots),
        in_specs=[pl.BlockSpec(memory_space=pltpu.SMEM), vmem],
        out_specs=pl.BlockSpec(memory_space=pl.ANY),
        out_shape=jax.ShapeDtypeStruct(shape, BF16),
        scratch_shapes=[
            pltpu.VMEM(shape, BF16),
            pltpu.SemaphoreType.DMA((n_seq,)),
            pltpu.SemaphoreType.DMA((n_seq,)),
            pltpu.SemaphoreType.DMA,
        ],
        compiler_params=pltpu.CompilerParams(
            collective_id=1, has_side_effects=True, vmem_limit_bytes=VMEM_LIMIT
        ),
        name="swap_part",
    )(asked, normed)


GROUP = 4
SPAN = (KN + 1) * BL


def attend_kernel(
    place_ref, normed_ref, mid_ref, arrived_ref, w_q_ref, w_kv_ref, w_o_ref, out_ref,
    sources, keys_values, queries, attended,
):
    step = pl.program_id(0)
    for i in range(GROUP):
        sources[i * SPAN : i * SPAN + BL] = normed_ref[i * BL : (i + 1) * BL]
        for k in range(KN):
            start = i * SPAN + (k + 1) * BL
            spot = place_ref[(step * GROUP + i) * KN + k]
            sources[start : start + BL] = arrived_ref[spot]
    keys_values[...] = dot(sources[...], w_kv_ref[...]).astype(BF16)
    queries[...] = (
        dot(normed_ref[...], w_q_ref[...]).astype(BF16).astype(F32) * (1.0 / math.sqrt(P_SIZE))
    ).astype(BF16)
    first_half = lax.broadcasted_iota(jnp.int32, (BL, 128), 1) < P_SIZE

    for i in range(GROUP):
        for p in range(PAIRS):
            lanes = slice(p * 128, (p + 1) * 128)
            values = slice(INNER + p * 128, INNER + (p + 1) * 128)
            q = queries[i * BL : (i + 1) * BL, lanes]
            zero = jnp.zeros_like(q)
            q = jnp.concatenate(
                [jnp.where(first_half, q, zero), jnp.where(first_half, zero, q)], axis=0
            )
            score = dot_nt(q, keys_values[i * SPAN : (i + 1) * SPAN, lanes])
            raised = jnp.exp(score - jnp.max(score, axis=-1, keepdims=True))
            weight = raised * (1.0 / jnp.sum(raised, axis=-1, keepdims=True))
            mixed = dot(weight.astype(BF16), keys_values[i * SPAN : (i + 1) * SPAN, values])
            attended[i * BL : (i + 1) * BL, lanes] = jnp.where(
                first_half, mixed[:BL], mixed[BL:]
            ).astype(BF16)
    out_ref[...] = (mid_ref[...].astype(F32) + dot(attended[...], w_o_ref[...])).astype(BF16)


def attend_part(place, normed, mid, arrived, w_q, w_kv, w_o):
    count = normed.shape[0]
    tile = GROUP * BL
    whole = lambda *shape: pl.BlockSpec(shape, lambda i, place: (0,) * len(shape))
    return pl.pallas_call(
        attend_kernel,
        grid_spec=pltpu.PrefetchScalarGridSpec(
            num_scalar_prefetch=1,
            grid=(count // tile,),
            in_specs=[
                pl.BlockSpec((tile, 512), lambda i, place: (i, 0)),
                pl.BlockSpec((tile, 512), lambda i, place: (i, 0)),
                whole(*arrived.shape),
                whole(512, INNER),
                whole(512, 2 * INNER),
                whole(INNER, 512),
            ],
            out_specs=pl.BlockSpec((tile, 512), lambda i, place: (i, 0)),
            scratch_shapes=[
                pltpu.VMEM((GROUP * SPAN, 512), BF16),
                pltpu.VMEM((GROUP * SPAN, 2 * INNER), BF16),
                pltpu.VMEM((tile, INNER), BF16),
                pltpu.VMEM((tile, INNER), BF16),
            ],
        ),
        out_shape=jax.ShapeDtypeStruct((count, 512), BF16),
        compiler_params=pltpu.CompilerParams(vmem_limit_bytes=VMEM_LIMIT),
        name="attend_part",
    )(place, normed, mid, arrived, w_q, w_kv, w_o)


def per_device(
    n_grp, n_seq, tokens, norm_gain1, w_xz, w_bc, w_dt, dt_bias, decay_rate, curve_jump,
    skip_gain, norm_gain2, w_out, norm_gain3, w_q, w_kv, w_o, nbr_owner, nbr_block,
):
    count = tokens.shape[0]
    blocks = count // BL
    requests = blocks * KN
    slots = max(2, -(-requests // n_seq))
    owner = nbr_owner.reshape(-1)
    block = nbr_block.reshape(-1)
    order = jnp.arange(requests)
    earlier = (owner[:, None] == owner[None, :]) & (order[None, :] < order[:, None])
    rank = jnp.sum(earlier.astype(jnp.int32), axis=1)
    place = owner * slots + rank
    hit = place[None, :] == jnp.arange(n_seq * slots, dtype=jnp.int32)[:, None]
    wanted = jnp.sum(jnp.where(hit, block[None, :], 0), axis=1).reshape(n_seq, 1, slots)
    wanted = jnp.pad(wanted, ((0, 0), (0, 7), (0, 128 - slots)))

    xz, maps, intra, reach, state, factor, total, final = local_part(
        tokens, norm_gain1[None], w_xz, w_bc, w_dt, dt_bias[:, None], decay_rate[:, None],
        curve_jump.reshape(count // CH, 1, CH),
    )
    before, asked = prefix_part(final, total, wanted, n_grp, n_seq)
    mid, normed = finish_part(
        tokens, xz, maps, intra, reach, state, factor, before,
        jnp.repeat(skip_gain, P_SIZE)[None], norm_gain2[None], w_out, norm_gain3[None],
    )
    arrived = swap_part(asked[:, 0, :slots], normed.reshape(blocks, BL, 512), n_seq)
    return attend_part(
        place, normed, mid, arrived.reshape(n_seq * slots, BL, 512), w_q, w_kv, w_o
    )


def solution(mesh):
    shard = P(("grp", "seq"), None)
    in_specs = (
        shard, P(), P(), P(), P(), P(), P(), P(("grp", "seq")), P(), P(), P(), P(), P(), P(),
        P(), shard, shard,
    )
    body = functools.partial(per_device, mesh.shape["grp"], mesh.shape["seq"])
    return jax.shard_map(body, mesh=mesh, in_specs=in_specs, out_specs=shard, check_vma=False)
```

```python
import functools
import math

import jax
import jax.numpy as jnp
from jax import lax
from jax.experimental import pallas as pl
from jax.experimental.pallas import tpu as pltpu
from jax.sharding import PartitionSpec as P

H = 16
P_SIZE = 64
NS = 128
INNER = 1024
CH = 128
BL = 64
KN = 2
PAIRS = INNER // 128
ROWS = 16
EPS = 1e-05
VMEM_LIMIT = 56 * 1024 * 1024
MESH = pl.DeviceIdType.MESH
F32 = jnp.float32
BF16 = jnp.bfloat16


def dot(a, b):
    return jnp.dot(a, b, preferred_element_type=F32)


def dot_nt(a, b):
    return lax.dot_general(a, b, (((1,), (1,)), ((), ())), preferred_element_type=F32)


def dot_tn(a, b):
    return lax.dot_general(a, b, (((0,), (0,)), ((), ())), preferred_element_type=F32)


def rms_rows(values, weights):
    floats = values.astype(F32)
    scale = lax.rsqrt(jnp.mean(floats * floats, axis=-1, keepdims=True) + EPS)
    return (floats * scale * weights).astype(BF16)


def split3(values):
    high = values.astype(BF16)
    rest = values - high.astype(F32)
    middle = rest.astype(BF16)
    low = (rest - middle.astype(F32)).astype(BF16)
    return jnp.concatenate([high, middle, low], axis=0)


def head_spread():
    head = lax.broadcasted_iota(jnp.int32, (3 * H, INNER), 0) % H
    lane = lax.broadcasted_iota(jnp.int32, (3 * H, INNER), 1) // P_SIZE
    return (head == lane).astype(BF16)


def column(row):
    down = lax.broadcasted_iota(jnp.int32, (H, H), 0)
    along = lax.broadcasted_iota(jnp.int32, (H, H), 1)
    return jnp.sum(jnp.where(down == along, row, 0.0), axis=1, keepdims=True)


def local_kernel(
    tokens_ref, gain_ref, w_xz_ref, w_bc_ref, w_dt_ref, bias_ref, rate_ref, jump_ref,
    xz_ref, maps_ref, intra_ref, reach_ref, state_ref, factor_ref, total_ref, final_ref,
    carried, product,
):
    step = pl.program_id(0)
    chunks = tokens_ref.shape[0] // CH

    @pl.when(step == 0)
    def _():
        carried[...] = jnp.zeros_like(carried)
        product[...] = jnp.ones_like(product)

    normed = rms_rows(tokens_ref[...], gain_ref[...])
    xz_ref[...] = dot(normed, w_xz_ref[...]).astype(BF16)
    maps_ref[...] = dot(normed, w_bc_ref[...]).astype(BF16)
    steps_t = jax.nn.softplus(
        dot_nt(w_dt_ref[...], normed) + column(bias_ref[...])
    )
    rate = column(rate_ref[...])
    row = lax.broadcasted_iota(jnp.int32, (CH, CH), 0)
    col = lax.broadcasted_iota(jnp.int32, (CH, CH), 1)
    lower = row >= col
    upto = (row <= col).astype(F32)
    spread = head_spread()
    first_half = lax.broadcasted_iota(jnp.int32, (CH, 128), 1) < P_SIZE
    for c in range(chunks):
        rows = slice(c * CH, (c + 1) * CH)
        u_t = steps_t[:, rows]
        decay_t = -(rate * u_t + jump_ref[c])
        run_t = jnp.dot(decay_t, upto, precision=lax.Precision.HIGHEST, preferred_element_type=F32)
        run = jnp.concatenate([run_t, jnp.zeros((CH - H, CH), F32)], axis=0).T
        reach_t = jnp.exp(run_t)
        tail_t = jnp.exp(run_t[:, CH - 1 :] - run_t) * u_t
        reach_ref[:, rows] = reach_t
        tail_weight = dot_tn(split3(tail_t), spread)
        last = dot_tn(split3(reach_t[:, CH - 8 :]), spread)[7:8]
        b = maps_ref[rows, :NS]
        cmap = maps_ref[rows, NS:]
        crossing = dot_nt(cmap, b)
        for p in range(PAIRS):
            lanes = slice(p * 128, (p + 1) * 128)
            x = xz_ref[rows, lanes]
            parts = []
            for h in (2 * p, 2 * p + 1):
                gap = run[:, h : h + 1] - run_t[h : h + 1, :]
                weight = jnp.exp(jnp.where(lower, gap, -1e30))
                parts.append((crossing * weight * u_t[h : h + 1, :]).astype(BF16))
            zero = jnp.zeros_like(x)
            stacked = jnp.concatenate(
                [jnp.where(first_half, x, zero), jnp.where(first_half, zero, x)], axis=0
            )
            intra_ref[rows, lanes] = dot(jnp.concatenate(parts, axis=1), stacked)
        state_ref[c] = carried[...]
        factor_ref[c] = jnp.broadcast_to(product[...], (8, INNER))
        tail = (tail_weight * xz_ref[rows, :INNER].astype(F32)).astype(BF16)
        carried[...] = last * carried[...] + dot_tn(b, tail)
        product[...] = product[...] * last

    @pl.when(step == pl.num_programs(0) - 1)
    def _():
        final_ref[...] = carried[...].astype(BF16)
        for i in range(8):
            total_ref[i : i + 1, :] = product[:, i * 128 : (i + 1) * 128]


def local_part(tokens, gain, w_xz, w_bc, w_dt, bias, rate, jump):
    count = tokens.shape[0]
    tile = 2 * CH
    chunks = count // CH
    whole = lambda *shape: pl.BlockSpec(shape, lambda i: (0,) * len(shape))
    return pl.pallas_call(
        local_kernel,
        grid=(count // tile,),
        in_specs=[
            pl.BlockSpec((tile, 512), lambda i: (i, 0)),
            whole(1, 512),
            whole(512, 2 * INNER),
            whole(512, 2 * NS),
            whole(H, 512),
            whole(1, H),
            whole(1, H),
            pl.BlockSpec((2, 1, CH), lambda i: (i, 0, 0)),
        ],
        out_specs=[
            pl.BlockSpec((tile, 2 * INNER), lambda i: (i, 0)),
            pl.BlockSpec((tile, 2 * NS), lambda i: (i, 0)),
            pl.BlockSpec((tile, INNER), lambda i: (i, 0)),
            pl.BlockSpec((H, tile), lambda i: (0, i)),
            pl.BlockSpec((2, NS, INNER), lambda i: (i, 0, 0)),
            pl.BlockSpec((2, 8, INNER), lambda i: (i, 0, 0)),
            whole(8, 128),
            whole(NS, INNER),
        ],
        out_shape=[
            jax.ShapeDtypeStruct((count, 2 * INNER), BF16),
            jax.ShapeDtypeStruct((count, 2 * NS), BF16),
            jax.ShapeDtypeStruct((count, INNER), F32),
            jax.ShapeDtypeStruct((H, count), F32),
            jax.ShapeDtypeStruct((chunks, NS, INNER), F32),
            jax.ShapeDtypeStruct((chunks, 8, INNER), F32),
            jax.ShapeDtypeStruct((8, 128), F32),
            jax.ShapeDtypeStruct((NS, INNER), BF16),
        ],
        scratch_shapes=[pltpu.VMEM((NS, INNER), F32), pltpu.VMEM((1, INNER), F32)],
        compiler_params=pltpu.CompilerParams(vmem_limit_bytes=VMEM_LIMIT),
        name="local_part",
    )(tokens, gain, w_xz, w_bc, w_dt, bias, rate, jump)


def greet(n_grp, n_seq, grp, seq):
    barrier = pltpu.get_barrier_semaphore()
    for d in range(1, n_seq):
        pl.semaphore_signal(
            barrier, inc=1, device_id=(grp, lax.rem(seq + d, n_seq)), device_id_type=MESH
        )
    for d in range(1, n_grp):
        pl.semaphore_signal(
            barrier, inc=1, device_id=(lax.rem(grp + d, n_grp), seq), device_id_type=MESH
        )
    pl.semaphore_wait(barrier, n_seq + n_grp - 2)


def prefix_kernel(
    n_grp, n_seq, state_ref, total_ref, wanted_ref, before_ref, asked_ref,
    parts, factors, sums, group_factor, shares, group_sum, my_factor, factor_row,
    send1, recv1, send2, recv2, send3, recv3, send4, recv4, send5, recv5, send6, recv6,
):
    grp, seq = lax.axis_index("grp"), lax.axis_index("seq")
    width = parts.shape[-1]
    greet(n_grp, n_seq, grp, seq)
    peers = [lax.rem(seq + d, n_seq) for d in range(n_seq)]
    origins = [lax.rem(seq + n_seq - d, n_seq) for d in range(n_seq)]
    layers = [lax.rem(grp + d, n_grp) for d in range(n_grp)]

    def across(src, dst, send, recv, d):
        return pltpu.make_async_remote_copy(
            src_ref=src, dst_ref=dst, send_sem=send.at[d], recv_sem=recv.at[d],
            device_id=(grp, peers[d]), device_id_type=MESH,
        )

    def along(src, dst, send, recv, d):
        return pltpu.make_async_remote_copy(
            src_ref=src, dst_ref=dst, send_sem=send.at[d], recv_sem=recv.at[d],
            device_id=(layers[d], seq), device_id_type=MESH,
        )

    first = []
    for d in range(1, n_seq):
        first.append(across(state_ref.at[peers[d]], parts.at[seq], send1, recv1, d))
        first.append(across(total_ref, factors.at[seq], send2, recv2, d))
    for copy in first:
        copy.start()
    asking = []
    for d in range(1, n_seq):
        asking.append(across(wanted_ref.at[peers[d]], asked_ref.at[seq], send3, recv3, d))
        asking[-1].start()
    parts[seq] = state_ref[seq]
    factors[seq] = total_ref[...]
    asked_ref[seq] = wanted_ref[seq]
    for copy in first:
        copy.wait()

    lanes = pl.ds(pl.multiple_of(lax.rem(seq, INNER // width) * width, width), width)

    def row_of(tile):
        for i in range(8):
            factor_row[:, i * 128 : (i + 1) * 128] = tile[i : i + 1, :]
        return factor_row[:, lanes]

    running = jnp.zeros((ROWS, width), F32)
    product = jnp.ones((8, 128), F32)
    for k in range(n_seq):
        sums[k] = running
        group_factor[k] = product
        running = row_of(factors[k]) * running + parts[k].astype(F32)
        product = product * factors[k]
    group_sum[grp] = running.astype(BF16)
    my_factor[grp] = product
    second = []
    for d in range(1, n_grp):
        second.append(along(group_sum.at[grp], group_sum.at[grp], send4, recv4, d))
        second.append(along(my_factor.at[grp], my_factor.at[grp], send5, recv5, d))
    for copy in second:
        copy.start()
    for copy in second:
        copy.wait()
    carry = jnp.zeros((ROWS, width), F32)
    for g in range(n_grp):
        new = row_of(my_factor[g]) * carry + group_sum[g].astype(F32)
        carry = jnp.where(g < grp, new, carry)
    for k in range(n_seq):
        shares[k] = (sums[k] + row_of(group_factor[k]) * carry).astype(BF16)
    third = []
    for d in range(1, n_seq):
        third.append(across(shares.at[peers[d]], before_ref.at[seq], send6, recv6, d))
        third[-1].start()
    before_ref[seq] = shares[seq]
    for copy in third:
        copy.wait()
    for copy in asking:
        copy.wait()


def prefix_part(state, total, wanted, n_grp, n_seq):
    spots = n_seq // 8
    width = INNER // spots
    sliced = state.reshape(8, ROWS, spots, width).swapaxes(1, 2).reshape(n_seq, ROWS, width)
    vmem = pl.BlockSpec(memory_space=pltpu.VMEM)
    dma = pltpu.SemaphoreType.DMA
    before, asked = pl.pallas_call(
        functools.partial(prefix_kernel, n_grp, n_seq),
        in_specs=[vmem] * 3,
        out_specs=[vmem] * 2,
        out_shape=[
            jax.ShapeDtypeStruct((n_seq, ROWS, width), BF16),
            jax.ShapeDtypeStruct(wanted.shape, jnp.int32),
        ],
        scratch_shapes=[
            pltpu.VMEM((n_seq, ROWS, width), BF16),
            pltpu.VMEM((n_seq, 8, 128), F32),
            pltpu.VMEM((n_seq, ROWS, width), F32),
            pltpu.VMEM((n_seq, 8, 128), F32),
            pltpu.VMEM((n_seq, ROWS, width), BF16),
            pltpu.VMEM((n_grp, ROWS, width), BF16),
            pltpu.VMEM((n_grp, 8, 128), F32),
            pltpu.VMEM((1, INNER), F32),
        ]
        + [dma((n_seq,))] * 6
        + [dma((n_grp,))] * 4
        + [dma((n_seq,))] * 2,
        compiler_params=pltpu.CompilerParams(
            collective_id=0, has_side_effects=True, vmem_limit_bytes=VMEM_LIMIT
        ),
        name="prefix_part",
    )(sliced, total, wanted)
    before = before.reshape(8, spots, ROWS, width).swapaxes(1, 2).reshape(NS, INNER)
    return before, asked


def finish_kernel(
    tokens_ref, xz_ref, maps_ref, intra_ref, reach_ref, state_ref, factor_ref, before_ref,
    skip_ref, gain2_ref, w_out_ref, gain3_ref, mid_ref, normed_ref, scaled,
):
    chunks = tokens_ref.shape[0] // CH
    spread = head_spread()
    group = lax.broadcasted_iota(jnp.int32, (256, 256), 0) // P_SIZE
    other = lax.broadcasted_iota(jnp.int32, (256, 256), 1) // P_SIZE
    same = (group == other).astype(BF16)
    skip = dot_tn(split3(jnp.broadcast_to(column(skip_ref[...]), (H, 8))), spread)[0:1]
    for c in range(chunks):
        rows = slice(c * CH, (c + 1) * CH)
        state = state_ref[c] + factor_ref[c, 0:1] * before_ref[...].astype(F32)
        high = state.astype(BF16)
        low = (state - high.astype(F32)).astype(BF16)
        cmap = maps_ref[rows, NS:]
        reached = dot(
            jnp.concatenate([cmap, cmap], axis=1), jnp.concatenate([high, low], axis=0)
        )
        reach = dot_tn(split3(reach_ref[:, rows]), spread)
        mixed = intra_ref[rows] + reach * reached
        x = xz_ref[rows, :INNER].astype(F32)
        gate = xz_ref[rows, INNER:].astype(F32)
        gated = (mixed + skip * x) * (gate * jax.nn.sigmoid(gate))
        squares = (gated * gated).astype(BF16)
        power = jnp.concatenate(
            [dot(squares[:, i * 256 : (i + 1) * 256], same) for i in range(INNER // 256)], axis=1
        )
        scaled[rows] = (
            gated * lax.rsqrt(power * (1.0 / P_SIZE) + EPS) * gain2_ref[...]
        ).astype(BF16)
    middle = (tokens_ref[...].astype(F32) + dot(scaled[...], w_out_ref[...])).astype(BF16)
    mid_ref[...] = middle
    normed_ref[...] = rms_rows(middle, gain3_ref[...])


def finish_part(tokens, xz, maps, intra, reach, state, factor, before, skip, gain2, w_out, gain3):
    count = tokens.shape[0]
    tile = 2 * CH
    whole = lambda *shape: pl.BlockSpec(shape, lambda i: (0,) * len(shape))
    return pl.pallas_call(
        finish_kernel,
        grid=(count // tile,),
        in_specs=[
            pl.BlockSpec((tile, 512), lambda i: (i, 0)),
            pl.BlockSpec((tile, 2 * INNER), lambda i: (i, 0)),
            pl.BlockSpec((tile, 2 * NS), lambda i: (i, 0)),
            pl.BlockSpec((tile, INNER), lambda i: (i, 0)),
            pl.BlockSpec((H, tile), lambda i: (0, i)),
            pl.BlockSpec((2, NS, INNER), lambda i: (i, 0, 0)),
            pl.BlockSpec((2, 8, INNER), lambda i: (i, 0, 0)),
            whole(NS, INNER),
            whole(1, H),
            whole(1, INNER),
            whole(INNER, 512),
            whole(1, 512),
        ],
        out_specs=[pl.BlockSpec((tile, 512), lambda i: (i, 0))] * 2,
        out_shape=[jax.ShapeDtypeStruct((count, 512), BF16)] * 2,
        scratch_shapes=[pltpu.VMEM((tile, INNER), BF16)],
        compiler_params=pltpu.CompilerParams(vmem_limit_bytes=VMEM_LIMIT),
        name="finish_part",
    )(tokens, xz, maps, intra, reach, state, factor, before, skip, gain2, w_out, gain3)


SPAN = (KN + 1) * BL
QUADS = INNER // 256
PAIRED = 2


def attend_kernel(
    n_seq, slots, asked_ref, place_ref, normed_ref, mid_ref, w_q_hbm, w_kv_hbm, w_o_hbm, out_ref,
    w_q_ref, w_kv_ref, w_o_ref, staged, arrived, keys_values, queries, scores, attended,
    send, recv, loads,
):
    grp, seq = lax.axis_index("grp"), lax.axis_index("seq")
    blocks = normed_ref.shape[0]
    fetches = [
        pltpu.make_async_copy(src, dst, loads.at[i])
        for i, (src, dst) in enumerate(
            [(w_kv_hbm, w_kv_ref), (w_q_hbm, w_q_ref), (w_o_hbm, w_o_ref)]
        )
    ]
    for fetch in fetches:
        fetch.start()
    barrier = pltpu.get_barrier_semaphore()
    for d in range(1, n_seq):
        pl.semaphore_signal(
            barrier, inc=1, device_id=(grp, lax.rem(seq + d, n_seq)), device_id_type=MESH
        )
    pl.semaphore_wait(barrier, n_seq - 1)
    copies = []
    for d in range(1, n_seq):
        peer = lax.rem(seq + d, n_seq)
        for j in range(slots):
            staged[d, j] = normed_ref[asked_ref[peer, 0, j]]
        copies.append(
            pltpu.make_async_remote_copy(
                src_ref=staged.at[d], dst_ref=arrived.at[seq],
                send_sem=send.at[d], recv_sem=recv.at[d],
                device_id=(grp, peer), device_id_type=MESH,
            )
        )
        copies[-1].start()
    for fetch in fetches:
        fetch.wait()
    group = 4
    quarter = lax.broadcasted_iota(jnp.int32, (BL, 256), 1) // P_SIZE

    def own_blocks(t, carry):
        rows = normed_ref[pl.ds(t * group, group)].reshape(group * BL, 512)
        keys_values[pl.ds(t * group, group)] = (
            dot(rows, w_kv_ref[...]).astype(BF16).reshape(group, BL, 2 * INNER)
        )
        asking = (
            dot(rows, w_q_ref[...]).astype(BF16).astype(F32) * (1.0 / math.sqrt(P_SIZE))
        ).astype(BF16)
        for i in range(group):
            for u in range(QUADS):
                q = asking[i * BL : (i + 1) * BL, u * 256 : (u + 1) * 256]
                zero = jnp.zeros_like(q)
                queries[t * group + i, u] = jnp.concatenate(
                    [jnp.where(quarter == h, q, zero) for h in range(4)], axis=0
                )
        return carry

    lax.fori_loop(0, blocks // group, own_blocks, 0)
    for j in range(slots):
        keys_values[blocks + seq * slots + j] = keys_values[asked_ref[seq, 0, j]]
    for d in range(1, n_seq):
        origin = lax.rem(seq + n_seq - d, n_seq)
        copies[d - 1].wait_recv()
        rows = arrived[origin].reshape(slots * BL, 512)
        keys_values[pl.ds(blocks + origin * slots, slots)] = (
            dot(rows, w_kv_ref[...]).astype(BF16).reshape(slots, BL, 2 * INNER)
        )

    first_half = lax.broadcasted_iota(jnp.int32, (BL, 128), 1) < P_SIZE

    def attend(t, carry):
        units = [(i, u) for i in range(PAIRED) for u in range(QUADS)]
        spots = [
            [t * PAIRED + i]
            + [blocks + place_ref[k * blocks + t * PAIRED + i] for k in range(KN)]
            for i in range(PAIRED)
        ]

        def score(n):
            i, u = units[n]
            keys = jnp.concatenate(
                [keys_values[spot, :, u * 256 : (u + 1) * 256] for spot in spots[i]], axis=0
            )
            scores[n] = dot_nt(keys, queries[t * PAIRED + i, u])

        def mix(n):
            i, u = units[n]
            for half in range(2):
                lanes = slice(u * 256 + half * 128, u * 256 + (half + 1) * 128)
                values = slice(INNER + lanes.start, INNER + lanes.stop)
                part = scores[n, :, half * 128 : (half + 1) * 128]
                raised = jnp.exp(part - jnp.max(part, axis=0, keepdims=True))
                weight = raised * (1.0 / jnp.sum(raised, axis=0, keepdims=True))
                value = jnp.concatenate(
                    [keys_values[spot, :, values] for spot in spots[i]], axis=0
                )
                mixed = dot_tn(weight.astype(BF16), value)
                attended[pl.ds((t * PAIRED + i) * BL, BL), lanes] = jnp.where(
                    first_half, mixed[:BL], mixed[BL:]
                ).astype(BF16)

        ahead = 3
        for n in range(len(units) + ahead):
            if n < len(units):
                score(n)
            if n >= ahead:
                mix(n - ahead)
        return carry

    lax.fori_loop(0, blocks // PAIRED, attend, 0)

    def project(t, carry):
        rows = pl.ds(t * 256, 256)
        out_ref[rows] = (
            mid_ref[rows].astype(F32) + dot(attended[rows], w_o_ref[...])
        ).astype(BF16)
        return carry

    lax.fori_loop(0, blocks * BL // 256, project, 0)
    for copy in copies:
        copy.wait_send()


def attend_part(asked, place, normed, mid, w_q, w_kv, w_o, n_seq, slots):
    count = mid.shape[0]
    blocks = count // BL
    vmem = pl.BlockSpec(memory_space=pltpu.VMEM)
    smem = pl.BlockSpec(memory_space=pltpu.SMEM)
    anywhere = pl.BlockSpec(memory_space=pl.ANY)
    dma = pltpu.SemaphoreType.DMA
    return pl.pallas_call(
        functools.partial(attend_kernel, n_seq, slots),
        in_specs=[smem, smem, vmem, vmem, anywhere, anywhere, anywhere],
        out_specs=vmem,
        out_shape=jax.ShapeDtypeStruct((count, 512), BF16),
        scratch_shapes=[
            pltpu.VMEM(w_q.shape, BF16),
            pltpu.VMEM(w_kv.shape, BF16),
            pltpu.VMEM(w_o.shape, BF16),
            pltpu.VMEM((n_seq, slots, BL, 512), BF16),
            pltpu.VMEM((n_seq, slots, BL, 512), BF16),
            pltpu.VMEM((blocks + n_seq * slots, BL, 2 * INNER), BF16),
            pltpu.VMEM((blocks, QUADS, 256, 256), BF16),
            pltpu.VMEM((PAIRED * QUADS, SPAN, 256), F32),
            pltpu.VMEM((count, INNER), BF16),
            dma((n_seq,)),
            dma((n_seq,)),
            dma((3,)),
        ],
        compiler_params=pltpu.CompilerParams(
            collective_id=1, has_side_effects=True, vmem_limit_bytes=VMEM_LIMIT
        ),
        name="attend_part",
    )(asked, place, normed, mid, w_q, w_kv, w_o)


def per_device(
    n_grp, n_seq, tokens, norm_gain1, w_xz, w_bc, w_dt, dt_bias, decay_rate, curve_jump,
    skip_gain, norm_gain2, w_out, norm_gain3, w_q, w_kv, w_o, nbr_owner, nbr_block,
):
    count = tokens.shape[0]
    blocks = count // BL
    requests = blocks * KN
    slots = max(2, -(-requests // n_seq))
    owner = nbr_owner.T.reshape(-1)
    block = nbr_block.T.reshape(-1)
    order = jnp.arange(requests)
    earlier = (owner[:, None] == owner[None, :]) & (order[None, :] < order[:, None])
    rank = jnp.sum(earlier.astype(jnp.int32), axis=1)
    place = owner * slots + rank
    hit = place[None, :] == jnp.arange(n_seq * slots, dtype=jnp.int32)[:, None]
    wanted = jnp.sum(jnp.where(hit, block[None, :], 0), axis=1).reshape(n_seq, 1, slots)
    wanted = jnp.pad(wanted, ((0, 0), (0, 7), (0, 128 - slots)))

    xz, maps, intra, reach, state, factor, total, final = local_part(
        tokens, norm_gain1[None], w_xz, w_bc, w_dt.T, dt_bias[None], decay_rate[None],
        curve_jump.reshape(count // CH, 1, CH),
    )
    before, asked = prefix_part(final, total, wanted, n_grp, n_seq)
    mid, normed = finish_part(
        tokens, xz, maps, intra, reach, state, factor, before,
        skip_gain[None], norm_gain2[None], w_out, norm_gain3[None],
    )
    return attend_part(
        asked, place, normed.reshape(blocks, BL, 512), mid, w_q, w_kv, w_o, n_seq, slots
    )


def solution(mesh):
    shard = P(("grp", "seq"), None)
    in_specs = (
        shard, P(), P(), P(), P(), P(), P(), P(("grp", "seq")), P(), P(), P(), P(), P(), P(),
        P(), shard, shard,
    )
    body = functools.partial(per_device, mesh.shape["grp"], mesh.shape["seq"])
    return jax.shard_map(body, mesh=mesh, in_specs=in_specs, out_specs=shard, check_vma=False)
```

```python
import functools
import math

import jax
import jax.numpy as jnp
from jax import lax
from jax.experimental import pallas as pl
from jax.experimental.pallas import tpu as pltpu
from jax.sharding import PartitionSpec as P

H = 16
P_SIZE = 64
NS = 128
INNER = 1024
CH = 128
BL = 64
KN = 2
PAIRS = INNER // 128
ROWS = 16
SPAN = (KN + 1) * BL
QUADS = INNER // 256
PAIRED = 2
EPS = 1e-05
VMEM_LIMIT = 60 * 1024 * 1024
MESH = pl.DeviceIdType.MESH
F32 = jnp.float32
BF16 = jnp.bfloat16


def dot(a, b):
    return jnp.dot(a, b, preferred_element_type=F32)


def dot_nt(a, b):
    return lax.dot_general(a, b, (((1,), (1,)), ((), ())), preferred_element_type=F32)


def dot_tn(a, b):
    return lax.dot_general(a, b, (((0,), (0,)), ((), ())), preferred_element_type=F32)


def rms_rows(values, weights):
    floats = values.astype(F32)
    scale = lax.rsqrt(jnp.mean(floats * floats, axis=-1, keepdims=True) + EPS)
    return (floats * scale * weights).astype(BF16)


def split3(values):
    high = values.astype(BF16)
    rest = values - high.astype(F32)
    middle = rest.astype(BF16)
    low = (rest - middle.astype(F32)).astype(BF16)
    return jnp.concatenate([high, middle, low], axis=0)


def head_spread():
    head = lax.broadcasted_iota(jnp.int32, (3 * H, INNER), 0) % H
    lane = lax.broadcasted_iota(jnp.int32, (3 * H, INNER), 1) // P_SIZE
    return (head == lane).astype(BF16)


def column(row):
    down = lax.broadcasted_iota(jnp.int32, (H, H), 0)
    along = lax.broadcasted_iota(jnp.int32, (H, H), 1)
    return jnp.sum(jnp.where(down == along, row, 0.0), axis=1, keepdims=True)


def int_column(row):
    size = row.shape[1]
    down = lax.broadcasted_iota(jnp.int32, (size, size), 0)
    along = lax.broadcasted_iota(jnp.int32, (size, size), 1)
    return jnp.sum(jnp.where(down == along, row, 0), axis=1, keepdims=True)


def request_lists(n_seq, slots, owner_ref, block_ref, wanted, place):
    blocks = owner_ref.shape[1]
    down = lax.broadcasted_iota(jnp.int32, (blocks, blocks), 0)
    along = lax.broadcasted_iota(jnp.int32, (blocks, blocks), 1)
    rows = [owner_ref[k : k + 1, :] for k in range(KN)]
    columns = [int_column(row) for row in rows]
    places = []
    for k in range(KN):
        rank = jnp.sum(
            jnp.where((columns[k] == rows[k]) & (down < along), 1, 0), axis=0, keepdims=True
        )
        for j in range(k):
            rank = rank + jnp.sum(
                jnp.where(columns[j] == rows[k], 1, 0), axis=0, keepdims=True
            )
        places.append(rows[k] * slots + rank)
        place[k : k + 1, :blocks] = places[k]
    slot = lax.broadcasted_iota(jnp.int32, (8, blocks), 0)
    for p in range(n_seq):
        named = jnp.zeros((8, 1), jnp.int32)
        for k in range(KN):
            hit = (places[k] == slot + p * slots) & (slot < slots)
            named = named + jnp.sum(
                jnp.where(hit, block_ref[k : k + 1, :], 0), axis=1, keepdims=True
            )
        wanted[p] = jnp.broadcast_to(named, (8, 128))


def layer_kernel(
    n_grp, n_seq, slots,
    tokens_ref, gain_ref, w_bc_ref, w_dt_ref, bias_ref, rate_ref, jump_ref, skip_ref,
    gain2_ref, gain3_ref, owner_ref, block_ref,
    w_xz_hbm, w_out_hbm, w_q_hbm, w_kv_hbm, w_o_hbm,
    out_ref,
    w_xz_ref, w_out_ref, w_q_ref, w_kv_ref, w_o_ref,
    xz_ref, maps_ref, pre_ref, state_ref, step_ref, run_ref, base_ref, carried,
    mid_ref, normed_ref, queries, scores,
    final, total, wanted, asked, asked_here, place, place_here,
    parts, factors, sums, group_factor, shares, group_sum, my_factor, before_ref, factor_row,
    staged, arrived, keys_values,
    loads, small, send1, recv1, send2, recv2, send3, recv3, send6, recv6, send, recv,
    send4, recv4, send5, recv5,
):
    grp, seq = lax.axis_index("grp"), lax.axis_index("seq")
    barrier = pltpu.get_barrier_semaphore()
    for d in range(1, n_seq):
        pl.semaphore_signal(
            barrier, inc=1, device_id=(grp, lax.rem(seq + d, n_seq)), device_id_type=MESH
        )
    for d in range(1, n_grp):
        pl.semaphore_signal(
            barrier, inc=1, device_id=(lax.rem(grp + d, n_grp), seq), device_id_type=MESH
        )
    fetches = [
        pltpu.make_async_copy(src, dst, loads.at[i])
        for i, (src, dst) in enumerate(
            [
                (w_xz_hbm, w_xz_ref), (w_out_hbm, w_out_ref), (w_kv_hbm, w_kv_ref),
                (w_q_hbm, w_q_ref), (w_o_hbm, w_o_ref),
            ]
        )
    ]
    for fetch in fetches:
        fetch.start()
    place[...] = jnp.zeros_like(place)
    request_lists(n_seq, slots, owner_ref, block_ref, wanted, place)
    placing = pltpu.make_async_copy(place, place_here, small.at[0])
    placing.start()

    count = tokens_ref.shape[0]
    blocks = normed_ref.shape[0]
    chunks = count // CH
    spread = head_spread()
    row = lax.broadcasted_iota(jnp.int32, (CH, CH), 0)
    col = lax.broadcasted_iota(jnp.int32, (CH, CH), 1)
    lower = row >= col
    upto = (row <= col).astype(F32)
    first_lanes = lax.broadcasted_iota(jnp.int32, (CH, 128), 1) < P_SIZE
    bias, rate = column(bias_ref[...]), column(rate_ref[...])
    skip = dot_tn(split3(jnp.broadcast_to(column(skip_ref[...]), (H, 8))), spread)[0:1]

    carried[...] = jnp.zeros_like(carried)
    fetches[0].wait()

    def states(t, base):
        start = pl.multiple_of(t * 2 * CH, 2 * CH)
        tile = pl.ds(start, 2 * CH)
        normed = rms_rows(tokens_ref[tile], gain_ref[...])
        stream = dot(normed, w_xz_ref[:, :INNER]).astype(BF16)
        xz_ref[tile, :INNER] = stream
        xz_ref[tile, INNER:] = dot(normed, w_xz_ref[:, INNER:]).astype(BF16)
        maps = dot(normed, w_bc_ref[...]).astype(BF16)
        maps_ref[tile] = maps
        steps_t = jax.nn.softplus(dot_nt(w_dt_ref[...], normed) + bias)
        for i in range(2):
            c = t * 2 + i
            rows = slice(i * CH, (i + 1) * CH)
            u_t = steps_t[:, rows]
            decay_t = -(rate * u_t + jump_ref[c])
            run_t = jnp.dot(
                decay_t, upto, precision=lax.Precision.HIGHEST, preferred_element_type=F32
            )
            step_ref[c] = u_t
            run_ref[c] = run_t
            base_ref[c] = run_t + base
            ending = run_t[:, CH - 1 :]
            tail_t = jnp.exp(ending - run_t) * u_t
            tail_weight = dot_tn(split3(tail_t), spread)
            last = dot_tn(split3(jnp.broadcast_to(jnp.exp(ending), (H, 8))), spread)[0:1]
            state = carried[...]
            high = state.astype(BF16)
            state_ref[c, :NS] = high
            state_ref[c, NS:] = (state - high.astype(F32)).astype(BF16)
            tail = (tail_weight * stream[rows].astype(F32)).astype(BF16)
            carried[...] = last * state + dot_tn(maps[rows, :NS], tail)
            base = base + ending
        return base

    base = lax.fori_loop(0, chunks // 2, states, jnp.zeros((H, 1), F32))
    width = parts.shape[-1]
    spots = INNER // width
    for k in range(n_seq):
        down, across_lanes = k // spots, k % spots
        final[k] = carried[
            down * ROWS : (down + 1) * ROWS, across_lanes * width : (across_lanes + 1) * width
        ].astype(BF16)
    product = dot_tn(split3(jnp.broadcast_to(jnp.exp(base), (H, 8))), spread)[0:1]
    for i in range(8):
        total[i : i + 1, :] = product[:, i * 128 : (i + 1) * 128]

    def mix_block(c, carry):
        rows = pl.ds(pl.multiple_of(c * CH, CH), CH)
        run_t, u_t = run_ref[c], step_ref[c]
        run = jnp.concatenate([run_t, jnp.zeros((CH - H, CH), F32)], axis=0).T
        cmap = maps_ref[rows, NS:]
        crossing = dot_nt(cmap, maps_ref[rows, :NS])
        reach = dot_tn(split3(jnp.exp(run_t)), spread)
        reached = dot(jnp.concatenate([cmap, cmap], axis=1), state_ref[c])
        for p in range(PAIRS):
            lanes = slice(p * 128, (p + 1) * 128)
            x = xz_ref[rows, lanes]
            pieces = []
            for h in (2 * p, 2 * p + 1):
                gap = run[:, h : h + 1] - run_t[h : h + 1, :]
                weight = jnp.exp(jnp.where(lower, gap, -1e30))
                pieces.append((crossing * weight * u_t[h : h + 1, :]).astype(BF16))
            zero = jnp.zeros_like(x)
            stacked = jnp.concatenate(
                [jnp.where(first_lanes, x, zero), jnp.where(first_lanes, zero, x)], axis=0
            )
            pre_ref[rows, lanes] = (
                dot(jnp.concatenate(pieces, axis=1), stacked)
                + reach[:, lanes] * reached[:, lanes]
                + skip[:, lanes] * x.astype(F32)
            )
        return carry

    pl.semaphore_wait(barrier, n_seq + n_grp - 2)
    peers = [lax.rem(seq + d, n_seq) for d in range(n_seq)]
    layers = [lax.rem(grp + d, n_grp) for d in range(n_grp)]

    def across(src, dst, sender, receiver, d):
        return pltpu.make_async_remote_copy(
            src_ref=src, dst_ref=dst, send_sem=sender.at[d], recv_sem=receiver.at[d],
            device_id=(grp, peers[d]), device_id_type=MESH,
        )

    def along(src, dst, sender, receiver, d):
        return pltpu.make_async_remote_copy(
            src_ref=src, dst_ref=dst, send_sem=sender.at[d], recv_sem=receiver.at[d],
            device_id=(layers[d], seq), device_id_type=MESH,
        )

    first = []
    for d in range(1, n_seq):
        first.append(across(final.at[peers[d]], parts.at[seq], send1, recv1, d))
        first.append(across(total, factors.at[seq], send2, recv2, d))
    for copy in first:
        copy.start()
    asking = []
    for d in range(1, n_seq):
        asking.append(across(wanted.at[peers[d]], asked.at[seq], send3, recv3, d))
        asking[-1].start()
    parts[seq] = final[seq]
    factors[seq] = total[...]
    asked[seq] = wanted[seq]

    lax.fori_loop(0, chunks // 2, mix_block, 0)
    for copy in first:
        copy.wait()
    lanes_here = pl.ds(pl.multiple_of(lax.rem(seq, spots) * width, width), width)

    def row_of(tile):
        for i in range(8):
            factor_row[:, i * 128 : (i + 1) * 128] = tile[i : i + 1, :]
        return factor_row[:, lanes_here]

    running = jnp.zeros((ROWS, width), F32)
    product = jnp.ones((8, 128), F32)
    for k in range(n_seq):
        sums[k] = running
        group_factor[k] = product
        running = row_of(factors[k]) * running + parts[k].astype(F32)
        product = product * factors[k]
    group_sum[grp] = running.astype(BF16)
    my_factor[grp] = product
    second = []
    for d in range(1, n_grp):
        second.append(along(group_sum.at[grp], group_sum.at[grp], send4, recv4, d))
        second.append(along(my_factor.at[grp], my_factor.at[grp], send5, recv5, d))
    for copy in second:
        copy.start()
    for copy in asking:
        copy.wait()
    listing = pltpu.make_async_copy(asked, asked_here, small.at[1])
    listing.start()
    lax.fori_loop(chunks // 2, 3 * chunks // 4, mix_block, 0)
    for copy in second:
        copy.wait()
    carry = jnp.zeros((ROWS, width), F32)
    for g in range(n_grp):
        new = row_of(my_factor[g]) * carry + group_sum[g].astype(F32)
        carry = jnp.where(g < grp, new, carry)
    for k in range(n_seq):
        shares[k] = (sums[k] + row_of(group_factor[k]) * carry).astype(BF16)
    third = []
    for d in range(1, n_seq):
        third.append(across(shares.at[peers[d]], before_ref.at[seq], send6, recv6, d))
        third[-1].start()
    before_ref[seq] = shares[seq]
    lax.fori_loop(3 * chunks // 4, chunks, mix_block, 0)
    for copy in third:
        copy.wait()
    listing.wait()
    placing.wait()
    for fetch in fetches[1:]:
        fetch.wait()

    group = lax.broadcasted_iota(jnp.int32, (256, 256), 0) // P_SIZE
    other = lax.broadcasted_iota(jnp.int32, (256, 256), 1) // P_SIZE
    same = (group == other).astype(BF16)

    def finish(t, carry):
        tile = pl.ds(pl.multiple_of(t * 2 * CH, 2 * CH), 2 * CH)
        before = jnp.concatenate(
            [
                jnp.concatenate([before_ref[a * spots + b] for b in range(spots)], axis=1)
                for a in range(NS // ROWS)
            ],
            axis=0,
        )
        entered = dot(maps_ref[tile, NS:], before)
        reach = jnp.concatenate(
            [dot_tn(split3(jnp.exp(base_ref[t * 2 + i])), spread) for i in range(2)], axis=0
        )
        mixed = pre_ref[tile] + reach * entered
        gate = xz_ref[tile, INNER:].astype(F32)
        gated = mixed * (gate * jax.nn.sigmoid(gate))
        squares = (gated * gated).astype(BF16)
        power = jnp.concatenate(
            [dot(squares[:, i * 256 : (i + 1) * 256], same) for i in range(INNER // 256)], axis=1
        )
        scaled = (gated * lax.rsqrt(power * (1.0 / P_SIZE) + EPS) * gain2_ref[...]).astype(BF16)
        middle = (tokens_ref[tile].astype(F32) + dot(scaled, w_out_ref[...])).astype(BF16)
        mid_ref[tile] = middle
        normed_ref[pl.ds(t * 4, 4)] = rms_rows(middle, gain3_ref[...]).reshape(4, BL, 512)
        return carry

    lax.fori_loop(0, chunks // 2, finish, 0)
    copies = []
    for d in range(1, n_seq):
        for j in range(slots):
            staged[d, j] = normed_ref[asked_here[peers[d], j, 0]]
        copies.append(across(staged.at[d], arrived.at[seq], send, recv, d))
        copies[-1].start()
    group = 4
    quarter = lax.broadcasted_iota(jnp.int32, (BL, 256), 1) // P_SIZE

    def own_blocks(t, carry):
        rows = normed_ref[pl.ds(t * group, group)].reshape(group * BL, 512)
        keys_values[pl.ds(t * group, group)] = (
            dot(rows, w_kv_ref[...]).astype(BF16).reshape(group, BL, 2 * INNER)
        )
        asking = (
            dot(rows, w_q_ref[...]).astype(BF16).astype(F32) * (1.0 / math.sqrt(P_SIZE))
        ).astype(BF16)
        queries[pl.ds(t * group, group)] = asking.reshape(group, BL, INNER)
        return carry

    lax.fori_loop(0, blocks // group, own_blocks, 0)
    for j in range(slots):
        keys_values[blocks + seq * slots + j] = keys_values[asked_here[seq, j, 0]]
    for d in range(1, n_seq):
        origin = lax.rem(seq + n_seq - d, n_seq)
        copies[d - 1].wait_recv()
        rows = arrived[origin].reshape(slots * BL, 512)
        keys_values[pl.ds(blocks + origin * slots, slots)] = (
            dot(rows, w_kv_ref[...]).astype(BF16).reshape(slots, BL, 2 * INNER)
        )

    first_half = lax.broadcasted_iota(jnp.int32, (BL, 128), 1) < P_SIZE

    def attend(t, carry):
        units = [(i, u) for i in range(PAIRED) for u in range(QUADS)]
        spots = [
            [t * PAIRED + i]
            + [blocks + place_here[k, t * PAIRED + i] for k in range(KN)]
            for i in range(PAIRED)
        ]

        def score(n):
            i, u = units[n]
            keys = jnp.concatenate(
                [keys_values[spot, :, u * 256 : (u + 1) * 256] for spot in spots[i]], axis=0
            )
            q = queries[t * PAIRED + i, :, u * 256 : (u + 1) * 256]
            zero = jnp.zeros_like(q)
            q = jnp.concatenate([jnp.where(quarter == h, q, zero) for h in range(4)], axis=0)
            scores[n] = dot_nt(keys, q)

        def mix(n):
            i, u = units[n]
            for half in range(2):
                lanes = slice(u * 256 + half * 128, u * 256 + (half + 1) * 128)
                values = slice(INNER + lanes.start, INNER + lanes.stop)
                part = scores[n, :, half * 128 : (half + 1) * 128]
                raised = jnp.exp(part - jnp.max(part, axis=0, keepdims=True))
                weight = raised * (1.0 / jnp.sum(raised, axis=0, keepdims=True))
                value = jnp.concatenate(
                    [keys_values[spot, :, values] for spot in spots[i]], axis=0
                )
                mixed = dot_tn(weight.astype(BF16), value)
                xz_ref[pl.ds((t * PAIRED + i) * BL, BL), lanes] = jnp.where(
                    first_half, mixed[:BL], mixed[BL:]
                ).astype(BF16)

        ahead = 3
        for n in range(len(units) + ahead):
            if n < len(units):
                score(n)
            if n >= ahead:
                mix(n - ahead)
        return carry

    lax.fori_loop(0, blocks // PAIRED, attend, 0)

    def project(t, carry):
        rows = pl.ds(t * 256, 256)
        out_ref[rows] = (
            mid_ref[rows].astype(F32) + dot(xz_ref[rows, :INNER], w_o_ref[...])
        ).astype(BF16)
        return carry

    lax.fori_loop(0, blocks * BL // 256, project, 0)
    for copy in copies:
        copy.wait_send()


def layer_part(
    n_grp, n_seq, tokens, norm_gain1, w_xz, w_bc, w_dt, dt_bias, decay_rate, curve_jump,
    skip_gain, norm_gain2, w_out, norm_gain3, w_q, w_kv, w_o, nbr_owner, nbr_block,
):
    count = tokens.shape[0]
    blocks, chunks = count // BL, count // CH
    slots = max(2, -(-blocks * KN // n_seq))
    width = INNER // (n_seq // 8)
    vmem = pl.BlockSpec(memory_space=pltpu.VMEM)
    anywhere = pl.BlockSpec(memory_space=pl.ANY)
    dma = pltpu.SemaphoreType.DMA
    held = [
        (w_xz.shape, BF16), (w_out.shape, BF16), (w_q.shape, BF16), (w_kv.shape, BF16),
        (w_o.shape, BF16),
        ((count, 2 * INNER), BF16), ((count, 2 * NS), BF16), ((count, INNER), F32),
        ((chunks, 2 * NS, INNER), BF16), ((chunks, H, CH), F32), ((chunks, H, CH), F32),
        ((chunks, H, CH), F32), ((NS, INNER), F32),
        ((count, 512), BF16), ((blocks, BL, 512), BF16), ((blocks, BL, INNER), BF16),
        ((PAIRED * QUADS, SPAN, 256), F32),
        ((n_seq, ROWS, width), BF16), ((8, 128), F32), ((n_seq, 8, 128), jnp.int32),
        ((n_seq, 8, 128), jnp.int32), None, ((8, 128), jnp.int32), None,
        ((n_seq, ROWS, width), BF16), ((n_seq, 8, 128), F32), ((n_seq, ROWS, width), F32),
        ((n_seq, 8, 128), F32), ((n_seq, ROWS, width), BF16), ((n_grp, ROWS, width), BF16),
        ((n_grp, 8, 128), F32), ((n_seq, ROWS, width), BF16), ((1, INNER), F32),
        ((n_seq, slots, BL, 512), BF16), ((n_seq, slots, BL, 512), BF16),
        ((blocks + n_seq * slots, BL, 2 * INNER), BF16),
    ]
    scratch = [pltpu.VMEM(*item) if item else None for item in held]
    scratch[21] = pltpu.SMEM((n_seq, 8, 128), jnp.int32)
    scratch[23] = pltpu.SMEM((8, 128), jnp.int32)
    return pl.pallas_call(
        functools.partial(layer_kernel, n_grp, n_seq, slots),
        in_specs=[vmem] * 12 + [anywhere] * 5,
        out_specs=vmem,
        out_shape=jax.ShapeDtypeStruct((count, 512), BF16),
        scratch_shapes=scratch
        + [dma((5,)), dma((2,))]
        + [dma((n_seq,))] * 10
        + [dma((n_grp,))] * 4,
        compiler_params=pltpu.CompilerParams(
            collective_id=0, has_side_effects=True, vmem_limit_bytes=VMEM_LIMIT
        ),
        name="layer_part",
    )(
        tokens, norm_gain1[None], w_bc, w_dt.T, dt_bias[None], decay_rate[None],
        curve_jump.reshape(chunks, 1, CH), skip_gain[None], norm_gain2[None], norm_gain3[None],
        nbr_owner.T, nbr_block.T, w_xz, w_out, w_q, w_kv, w_o,
    )


def solution(mesh):
    shard = P(("grp", "seq"), None)
    in_specs = (
        shard, P(), P(), P(), P(), P(), P(), P(("grp", "seq")), P(), P(), P(), P(), P(), P(),
        P(), shard, shard,
    )
    body = functools.partial(layer_part, mesh.shape["grp"], mesh.shape["seq"])
    return jax.shard_map(body, mesh=mesh, in_specs=in_specs, out_specs=shard, check_vma=False)
```

```python
import functools
import math

import jax
import jax.numpy as jnp
from jax import lax
from jax.experimental import pallas as pl
from jax.experimental.pallas import tpu as pltpu
from jax.sharding import PartitionSpec as P

H = 16
P_SIZE = 64
NS = 128
INNER = 1024
CH = 128
BL = 64
KN = 2
PAIRS = INNER // 128
ROWS = 16
SPAN = (KN + 1) * BL
QUADS = INNER // 256
PAIRED = 2
EPS = 1e-05
VMEM_LIMIT = 62 * 1024 * 1024
MESH = pl.DeviceIdType.MESH
F32 = jnp.float32
BF16 = jnp.bfloat16


def dot(a, b):
    return jnp.dot(a, b, preferred_element_type=F32)


def dot_nt(a, b):
    return lax.dot_general(a, b, (((1,), (1,)), ((), ())), preferred_element_type=F32)


def dot_tn(a, b):
    return lax.dot_general(a, b, (((0,), (0,)), ((), ())), preferred_element_type=F32)


def rms_rows(values, weights):
    floats = values.astype(F32)
    scale = lax.rsqrt(jnp.mean(floats * floats, axis=-1, keepdims=True) + EPS)
    return (floats * scale * weights).astype(BF16)


def split3(values):
    high = values.astype(BF16)
    rest = values - high.astype(F32)
    middle = rest.astype(BF16)
    low = (rest - middle.astype(F32)).astype(BF16)
    return jnp.concatenate([high, middle, low], axis=0)


def head_spread():
    head = lax.broadcasted_iota(jnp.int32, (3 * H, INNER), 0) % H
    lane = lax.broadcasted_iota(jnp.int32, (3 * H, INNER), 1) // P_SIZE
    return (head == lane).astype(BF16)


def column(row):
    down = lax.broadcasted_iota(jnp.int32, (H, H), 0)
    along = lax.broadcasted_iota(jnp.int32, (H, H), 1)
    return jnp.sum(jnp.where(down == along, row, 0.0), axis=1, keepdims=True)


def int_column(row):
    size = row.shape[1]
    down = lax.broadcasted_iota(jnp.int32, (size, size), 0)
    along = lax.broadcasted_iota(jnp.int32, (size, size), 1)
    return jnp.sum(jnp.where(down == along, row, 0), axis=1, keepdims=True)


def request_lists(n_seq, slots, owner_ref, block_ref, wanted, place):
    blocks = owner_ref.shape[1]
    down = lax.broadcasted_iota(jnp.int32, (blocks, blocks), 0)
    along = lax.broadcasted_iota(jnp.int32, (blocks, blocks), 1)
    rows = [owner_ref[k : k + 1, :] for k in range(KN)]
    columns = [int_column(row) for row in rows]
    places = []
    for k in range(KN):
        rank = jnp.sum(
            jnp.where((columns[k] == rows[k]) & (down < along), 1, 0), axis=0, keepdims=True
        )
        for j in range(k):
            rank = rank + jnp.sum(
                jnp.where(columns[j] == rows[k], 1, 0), axis=0, keepdims=True
            )
        places.append(rows[k] * slots + rank)
        place[k : k + 1, :blocks] = places[k]
    slot = lax.broadcasted_iota(jnp.int32, (8, blocks), 0)
    for p in range(n_seq):
        named = jnp.zeros((8, 1), jnp.int32)
        for k in range(KN):
            hit = (places[k] == slot + p * slots) & (slot < slots)
            named = named + jnp.sum(
                jnp.where(hit, block_ref[k : k + 1, :], 0), axis=1, keepdims=True
            )
        wanted[p] = jnp.broadcast_to(named, (8, 128))


def layer_kernel(
    n_grp, n_seq, slots,
    tokens_ref, gain_ref, w_bc_ref, w_dt_ref, bias_ref, rate_ref, jump_ref, skip_ref,
    gain2_ref, gain3_ref, owner_ref, block_ref,
    w_xz_hbm, w_out_hbm, w_q_hbm, w_kv_hbm, w_o_hbm,
    out_ref,
    w_xz_ref, w_out_ref, w_q_ref, w_kv_ref, w_o_ref,
    xz_ref, maps_ref, pre_ref, state_ref, step_ref, run_ref, base_ref, carried,
    mid_ref, normed_ref, queries, scores,
    final, total, wanted, asked, asked_here, place, place_here,
    parts, factors, sums, group_factor, group_sum, my_factor, before_ref, factor_row,
    staged, arrived, keys_values,
    loads, small, send1, recv1, send2, recv2, send3, recv3, send6, recv6, send, recv,
    send4, recv4, send5, recv5,
):
    grp, seq = lax.axis_index("grp"), lax.axis_index("seq")
    barrier = pltpu.get_barrier_semaphore()
    for d in range(1, n_seq):
        pl.semaphore_signal(
            barrier, inc=1, device_id=(grp, lax.rem(seq + d, n_seq)), device_id_type=MESH
        )
    for d in range(1, n_grp):
        pl.semaphore_signal(
            barrier, inc=1, device_id=(lax.rem(grp + d, n_grp), seq), device_id_type=MESH
        )
    fetches = [
        pltpu.make_async_copy(src, dst, loads.at[i])
        for i, (src, dst) in enumerate(
            [
                (w_xz_hbm, w_xz_ref), (w_out_hbm, w_out_ref), (w_kv_hbm, w_kv_ref),
                (w_q_hbm, w_q_ref), (w_o_hbm, w_o_ref),
            ]
        )
    ]
    for fetch in fetches:
        fetch.start()
    place[...] = jnp.zeros_like(place)
    request_lists(n_seq, slots, owner_ref, block_ref, wanted, place)
    placing = pltpu.make_async_copy(place, place_here, small.at[0])
    placing.start()

    count = tokens_ref.shape[0]
    blocks = normed_ref.shape[0]
    chunks = count // CH
    spread = head_spread()
    row = lax.broadcasted_iota(jnp.int32, (CH, CH), 0)
    col = lax.broadcasted_iota(jnp.int32, (CH, CH), 1)
    lower = row >= col
    upto = (row <= col).astype(F32)
    first_lanes = lax.broadcasted_iota(jnp.int32, (CH, 128), 1) < P_SIZE
    bias, rate = column(bias_ref[...]), column(rate_ref[...])
    skip = dot_tn(split3(jnp.broadcast_to(column(skip_ref[...]), (H, 8))), spread)[0:1]

    carried[...] = jnp.zeros_like(carried)
    fetches[0].wait()

    def states(t, base):
        start = pl.multiple_of(t * 2 * CH, 2 * CH)
        tile = pl.ds(start, 2 * CH)
        normed = rms_rows(tokens_ref[tile], gain_ref[...])
        stream = dot(normed, w_xz_ref[:, :INNER]).astype(BF16)
        xz_ref[tile, :INNER] = stream
        xz_ref[tile, INNER:] = dot(normed, w_xz_ref[:, INNER:]).astype(BF16)
        maps = dot(normed, w_bc_ref[...]).astype(BF16)
        maps_ref[tile] = maps
        steps_t = jax.nn.softplus(dot_nt(w_dt_ref[...], normed) + bias)
        for i in range(2):
            c = t * 2 + i
            rows = slice(i * CH, (i + 1) * CH)
            u_t = steps_t[:, rows]
            decay_t = -(rate * u_t + jump_ref[c])
            run_t = jnp.dot(
                decay_t, upto, precision=lax.Precision.HIGHEST, preferred_element_type=F32
            )
            step_ref[c] = u_t
            run_ref[c] = run_t
            base_ref[c] = run_t + base
            ending = run_t[:, CH - 1 :]
            tail_t = jnp.exp(ending - run_t) * u_t
            tail_weight = dot_tn(split3(tail_t), spread)
            last = dot_tn(split3(jnp.broadcast_to(jnp.exp(ending), (H, 8))), spread)[0:1]
            state = carried[...]
            high = state.astype(BF16)
            state_ref[c, :NS] = high
            state_ref[c, NS:] = (state - high.astype(F32)).astype(BF16)
            tail = (tail_weight * stream[rows].astype(F32)).astype(BF16)
            carried[...] = last * state + dot_tn(maps[rows, :NS], tail)
            base = base + ending
        return base

    base = lax.fori_loop(0, chunks // 2, states, jnp.zeros((H, 1), F32))
    width = parts.shape[-1]
    spots = INNER // width
    for k in range(n_seq):
        down, across_lanes = k // spots, k % spots
        final[k] = carried[
            down * ROWS : (down + 1) * ROWS, across_lanes * width : (across_lanes + 1) * width
        ].astype(BF16)
    product = dot_tn(split3(jnp.broadcast_to(jnp.exp(base), (H, 8))), spread)[0:1]
    for i in range(8):
        total[i : i + 1, :] = product[:, i * 128 : (i + 1) * 128]

    def mix_block(c, carry):
        rows = pl.ds(pl.multiple_of(c * CH, CH), CH)
        run_t, u_t = run_ref[c], step_ref[c]
        run = jnp.concatenate([run_t, jnp.zeros((CH - H, CH), F32)], axis=0).T
        scores[c, :CH, :CH] = jnp.concatenate(
            [jnp.exp(base_ref[c]), jnp.zeros((CH - H, CH), F32)], axis=0
        ).T
        cmap = maps_ref[rows, NS:]
        crossing = dot_nt(cmap, maps_ref[rows, :NS])
        reach = dot_tn(split3(jnp.exp(run_t)), spread)
        reached = dot(jnp.concatenate([cmap, cmap], axis=1), state_ref[c])
        for p in range(PAIRS):
            lanes = slice(p * 128, (p + 1) * 128)
            x = xz_ref[rows, lanes]
            pieces = []
            for h in (2 * p, 2 * p + 1):
                gap = run[:, h : h + 1] - run_t[h : h + 1, :]
                weight = jnp.exp(jnp.where(lower, gap, -1e30))
                pieces.append((crossing * weight * u_t[h : h + 1, :]).astype(BF16))
            zero = jnp.zeros_like(x)
            stacked = jnp.concatenate(
                [jnp.where(first_lanes, x, zero), jnp.where(first_lanes, zero, x)], axis=0
            )
            pre_ref[rows, lanes] = (
                dot(jnp.concatenate(pieces, axis=1), stacked)
                + reach[:, lanes] * reached[:, lanes]
                + skip[:, lanes] * x.astype(F32)
            )
        return carry

    pl.semaphore_wait(barrier, n_seq + n_grp - 2)
    peers = [lax.rem(seq + d, n_seq) for d in range(n_seq)]
    layers = [lax.rem(grp + d, n_grp) for d in range(n_grp)]

    def across(src, dst, sender, receiver, d):
        return pltpu.make_async_remote_copy(
            src_ref=src, dst_ref=dst, send_sem=sender.at[d], recv_sem=receiver.at[d],
            device_id=(grp, peers[d]), device_id_type=MESH,
        )

    def along(src, dst, sender, receiver, d):
        return pltpu.make_async_remote_copy(
            src_ref=src, dst_ref=dst, send_sem=sender.at[d], recv_sem=receiver.at[d],
            device_id=(layers[d], seq), device_id_type=MESH,
        )

    first = []
    for d in range(1, n_seq):
        first.append(across(final.at[peers[d]], parts.at[seq], send1, recv1, d))
        first.append(across(total, factors.at[seq], send2, recv2, d))
    for copy in first:
        copy.start()
    asking = []
    for d in range(1, n_seq):
        asking.append(across(wanted.at[peers[d]], asked.at[seq], send3, recv3, d))
        asking[-1].start()
    parts[seq] = final[seq]
    factors[seq] = total[...]
    asked[seq] = wanted[seq]

    lax.fori_loop(0, 3 * chunks // 8, mix_block, 0)
    for copy in first:
        copy.wait()
    lanes_here = pl.ds(pl.multiple_of(lax.rem(seq, spots) * width, width), width)

    def row_of(tile):
        for i in range(8):
            factor_row[:, i * 128 : (i + 1) * 128] = tile[i : i + 1, :]
        return factor_row[:, lanes_here]

    running = jnp.zeros((ROWS, width), F32)
    product = jnp.ones((8, 128), F32)
    for k in range(n_seq):
        sums[k] = running
        group_factor[k] = product
        running = row_of(factors[k]) * running + parts[k].astype(F32)
        product = product * factors[k]
    group_sum[grp] = running.astype(BF16)
    my_factor[grp] = product
    second = []
    for d in range(1, n_grp):
        second.append(along(group_sum.at[grp], group_sum.at[grp], send4, recv4, d))
        second.append(along(my_factor.at[grp], my_factor.at[grp], send5, recv5, d))
    for copy in second:
        copy.start()
    for copy in asking:
        copy.wait()
    listing = pltpu.make_async_copy(asked, asked_here, small.at[1])
    listing.start()
    lax.fori_loop(3 * chunks // 8, 5 * chunks // 8, mix_block, 0)
    for copy in second:
        copy.wait()
    carry = jnp.zeros((ROWS, width), F32)
    for g in range(n_grp):
        new = row_of(my_factor[g]) * carry + group_sum[g].astype(F32)
        carry = jnp.where(g < grp, new, carry)
    for k in range(n_seq):
        final[k] = (sums[k] + row_of(group_factor[k]) * carry).astype(BF16)
    third = []
    for d in range(1, n_seq):
        third.append(across(final.at[peers[d]], before_ref.at[seq], send6, recv6, d))
        third[-1].start()
    before_ref[seq] = final[seq]
    lax.fori_loop(5 * chunks // 8, chunks, mix_block, 0)
    for copy in third:
        copy.wait()
    listing.wait()
    placing.wait()
    for fetch in fetches[1:]:
        fetch.wait()

    group = lax.broadcasted_iota(jnp.int32, (256, 256), 0) // P_SIZE
    other = lax.broadcasted_iota(jnp.int32, (256, 256), 1) // P_SIZE
    same = (group == other).astype(BF16)

    before = jnp.concatenate(
        [
            jnp.concatenate([before_ref[a * spots + b] for b in range(spots)], axis=1)
            for a in range(NS // ROWS)
        ],
        axis=0,
    )
    padded = jnp.concatenate([spread[:H], jnp.zeros((128 - H, INNER), BF16)], axis=0)
    padded = jnp.concatenate([padded, padded], axis=0)
    copies = []
    for q in range(BL // ROWS):
        within = slice(q * ROWS, (q + 1) * ROWS)

        def strip(ref, lanes):
            return jnp.concatenate(
                [ref[b * BL + q * ROWS : b * BL + (q + 1) * ROWS, lanes] for b in range(blocks)],
                axis=0,
            )

        entered = dot(strip(maps_ref, slice(NS, 2 * NS)), before)
        reach = jnp.concatenate(
            [
                scores[b // 2, b % 2 * BL + q * ROWS : b % 2 * BL + (q + 1) * ROWS, :128]
                for b in range(blocks)
            ],
            axis=0,
        )
        high = reach.astype(BF16)
        low = (reach - high.astype(F32)).astype(BF16)
        reach = dot(jnp.concatenate([high, low], axis=1), padded)
        mixed = strip(pre_ref, slice(0, INNER)) + reach * entered
        gate = strip(xz_ref, slice(INNER, 2 * INNER)).astype(F32)
        gated = mixed * (gate * jax.nn.sigmoid(gate))
        squares = (gated * gated).astype(BF16)
        power = jnp.concatenate(
            [dot(squares[:, i * 256 : (i + 1) * 256], same) for i in range(INNER // 256)], axis=1
        )
        scaled = (gated * lax.rsqrt(power * (1.0 / P_SIZE) + EPS) * gain2_ref[...]).astype(BF16)
        middle = strip(tokens_ref, slice(0, 512)).astype(F32) + dot(scaled, w_out_ref[...])
        middle = middle.astype(BF16)
        for b in range(blocks):
            mid_ref[b * BL + q * ROWS : b * BL + (q + 1) * ROWS] = middle[
                b * ROWS : (b + 1) * ROWS
            ]
        normed_ref[:, within] = rms_rows(middle, gain3_ref[...]).reshape(blocks, ROWS, 512)
        for d in range(1, n_seq):
            for j in range(slots):
                staged[q, d, j] = normed_ref[asked_here[peers[d], j, 0], within]
            copies.append(
                pltpu.make_async_remote_copy(
                    src_ref=staged.at[q, d], dst_ref=arrived.at[q, seq],
                    send_sem=send.at[q, d], recv_sem=recv.at[q, d],
                    device_id=(grp, peers[d]), device_id_type=MESH,
                )
            )
            copies[-1].start()
        for j in range(slots):
            arrived[q, seq, j] = normed_ref[asked_here[seq, j, 0], within]
    group = 4
    quarter = lax.broadcasted_iota(jnp.int32, (BL, 256), 1) // P_SIZE

    def own_blocks(t, carry):
        rows = normed_ref[pl.ds(t * group, group)].reshape(group * BL, 512)
        keys_values[pl.ds(t * group, group)] = (
            dot(rows, w_kv_ref[...]).astype(BF16).reshape(group, BL, 2 * INNER)
        )
        asking = (
            dot(rows, w_q_ref[...]).astype(BF16).astype(F32) * (1.0 / math.sqrt(P_SIZE))
        ).astype(BF16)
        queries[pl.ds(t * group, group)] = asking.reshape(group, BL, INNER)
        return carry

    lax.fori_loop(0, blocks // group, own_blocks, 0)
    for q in range(BL // ROWS):
        for d in range(1, n_seq):
            copies[q * (n_seq - 1) + d - 1].wait_recv()
        several = 16 // slots
        for part in range(n_seq // several):
            rows = arrived[q, part * several : (part + 1) * several].reshape(16 * ROWS, 512)
            keys_values[
                blocks + part * 16 : blocks + (part + 1) * 16, q * ROWS : (q + 1) * ROWS
            ] = dot(rows, w_kv_ref[...]).astype(BF16).reshape(16, ROWS, 2 * INNER)

    first_half = lax.broadcasted_iota(jnp.int32, (BL, 128), 1) < P_SIZE

    def attend(t, carry):
        units = [(i, u) for i in range(PAIRED) for u in range(QUADS)]
        spots = [
            [t * PAIRED + i]
            + [blocks + place_here[k, t * PAIRED + i] for k in range(KN)]
            for i in range(PAIRED)
        ]

        def score(n):
            i, u = units[n]
            keys = jnp.concatenate(
                [keys_values[spot, :, u * 256 : (u + 1) * 256] for spot in spots[i]], axis=0
            )
            q = queries[t * PAIRED + i, :, u * 256 : (u + 1) * 256]
            zero = jnp.zeros_like(q)
            q = jnp.concatenate([jnp.where(quarter == h, q, zero) for h in range(4)], axis=0)
            scores[n] = dot_nt(keys, q)

        def mix(n):
            i, u = units[n]
            for half in range(2):
                lanes = slice(u * 256 + half * 128, u * 256 + (half + 1) * 128)
                values = slice(INNER + lanes.start, INNER + lanes.stop)
                part = scores[n, :, half * 128 : (half + 1) * 128]
                raised = jnp.exp(part - jnp.max(part, axis=0, keepdims=True))
                weight = raised * (1.0 / jnp.sum(raised, axis=0, keepdims=True))
                value = jnp.concatenate(
                    [keys_values[spot, :, values] for spot in spots[i]], axis=0
                )
                mixed = dot_tn(weight.astype(BF16), value)
                xz_ref[pl.ds((t * PAIRED + i) * BL, BL), lanes] = jnp.where(
                    first_half, mixed[:BL], mixed[BL:]
                ).astype(BF16)

        ahead = 3
        for n in range(len(units) + ahead):
            if n < len(units):
                score(n)
            if n >= ahead:
                mix(n - ahead)
        return carry

    lax.fori_loop(0, blocks // PAIRED, attend, 0)

    def project(t, carry):
        rows = pl.ds(t * 256, 256)
        out_ref[rows] = (
            mid_ref[rows].astype(F32) + dot(xz_ref[rows, :INNER], w_o_ref[...])
        ).astype(BF16)
        return carry

    lax.fori_loop(0, blocks * BL // 256, project, 0)
    for copy in copies:
        copy.wait_send()


def layer_part(
    n_grp, n_seq, tokens, norm_gain1, w_xz, w_bc, w_dt, dt_bias, decay_rate, curve_jump,
    skip_gain, norm_gain2, w_out, norm_gain3, w_q, w_kv, w_o, nbr_owner, nbr_block,
):
    count = tokens.shape[0]
    blocks, chunks = count // BL, count // CH
    slots = max(2, -(-blocks * KN // n_seq))
    width = INNER // (n_seq // 8)
    vmem = pl.BlockSpec(memory_space=pltpu.VMEM)
    anywhere = pl.BlockSpec(memory_space=pl.ANY)
    dma = pltpu.SemaphoreType.DMA
    held = [
        (w_xz.shape, BF16), (w_out.shape, BF16), (w_q.shape, BF16), (w_kv.shape, BF16),
        (w_o.shape, BF16),
        ((count, 2 * INNER), BF16), ((count, 2 * NS), BF16), ((count, INNER), F32),
        ((chunks, 2 * NS, INNER), BF16), ((chunks, H, CH), F32), ((chunks, H, CH), F32),
        ((chunks, H, CH), F32), ((NS, INNER), F32),
        ((count, 512), BF16), ((blocks, BL, 512), BF16), ((blocks, BL, INNER), BF16),
        ((PAIRED * QUADS, SPAN, 256), F32),
        ((n_seq, ROWS, width), BF16), ((8, 128), F32), ((n_seq, 8, 128), jnp.int32),
        ((n_seq, 8, 128), jnp.int32), None, ((8, 128), jnp.int32), None,
        ((n_seq, ROWS, width), BF16), ((n_seq, 8, 128), F32), ((n_seq, ROWS, width), F32),
        ((n_seq, 8, 128), F32), ((n_grp, ROWS, width), BF16),
        ((n_grp, 8, 128), F32), ((n_seq, ROWS, width), BF16), ((1, INNER), F32),
        ((BL // ROWS, n_seq, slots, ROWS, 512), BF16),
        ((BL // ROWS, n_seq, slots, ROWS, 512), BF16),
        ((blocks + n_seq * slots, BL, 2 * INNER), BF16),
    ]
    scratch = [pltpu.VMEM(*item) if item else None for item in held]
    scratch[21] = pltpu.SMEM((n_seq, 8, 128), jnp.int32)
    scratch[23] = pltpu.SMEM((8, 128), jnp.int32)
    return pl.pallas_call(
        functools.partial(layer_kernel, n_grp, n_seq, slots),
        in_specs=[vmem] * 12 + [anywhere] * 5,
        out_specs=vmem,
        out_shape=jax.ShapeDtypeStruct((count, 512), BF16),
        scratch_shapes=scratch
        + [dma((5,)), dma((2,))]
        + [dma((n_seq,))] * 8
        + [dma((BL // ROWS, n_seq))] * 2
        + [dma((n_grp,))] * 4,
        compiler_params=pltpu.CompilerParams(
            collective_id=0, has_side_effects=True, vmem_limit_bytes=VMEM_LIMIT
        ),
        name="layer_part",
    )(
        tokens, norm_gain1[None], w_bc, w_dt.T, dt_bias[None], decay_rate[None],
        curve_jump.reshape(chunks, 1, CH), skip_gain[None], norm_gain2[None], norm_gain3[None],
        nbr_owner.T, nbr_block.T, w_xz, w_out, w_q, w_kv, w_o,
    )


def solution(mesh):
    shard = P(("grp", "seq"), None)
    in_specs = (
        shard, P(), P(), P(), P(), P(), P(), P(("grp", "seq")), P(), P(), P(), P(), P(), P(),
        P(), shard, shard,
    )
    body = functools.partial(layer_part, mesh.shape["grp"], mesh.shape["seq"])
    return jax.shard_map(body, mesh=mesh, in_specs=in_specs, out_specs=shard, check_vma=False)
```
